256 devices in a mesh: dp: 16 (over x, y), tensor: 16 (over z, core).
Axes of the slice: x: 4, y: 4, z: 8, core: 2. Of those that a mesh axis runs over, the one named last changes fastest.
Arguments:
- tokens: bfloat16 [6144, 18432], P('dp', 'tensor'), may hold values from -6 to 6
- target: bfloat16 [6144, 18432], P('dp', 'tensor'), may hold values from -6 to 6
- first_in: float32 [512, 18432], P('dp', 'tensor'), may hold values from -0.046875 to 0.046875
- first_out: float32 [512, 36864], P('dp', 'tensor'), may hold values from -0.25 to 0.25
- second_in: float32 [512, 36864], P('dp', 'tensor'), may hold values from -0.03125 to 0.03125
- second_out: float32 [512, 18432], P('dp', 'tensor'), may hold values from -0.25 to 0.25
- width_mean: float32 [2, 512, 18432], P(None, 'dp', 'tensor'), may hold values from -0.00030517578 to 0.00030517578
- width_square: float32 [2, 512, 18432], P(None, 'dp', 'tensor'), may hold values from 1.7660635e-10 to 1.7660636e-08
- hidden_mean: float32 [2, 512, 36864], P(None, 'dp', 'tensor'), may hold values from -0.00030517578 to 0.00030517578
- hidden_square: float32 [2, 512, 36864], P(None, 'dp', 'tensor'), may hold values from 1.7660635e-10 to 1.7660636e-08
Outputs:
- new_first_in: float32 [512, 18432], P('dp', 'tensor')
- new_first_out: float32 [512, 36864], P('dp', 'tensor')
- new_second_in: float32 [512, 36864], P('dp', 'tensor')
- new_second_out: float32 [512, 18432], P('dp', 'tensor')
- new_width_mean: float32 [2, 512, 18432], P(None, 'dp', 'tensor')
- new_width_square: float32 [2, 512, 18432], P(None, 'dp', 'tensor')
- new_hidden_mean: float32 [2, 512, 36864], P(None, 'dp', 'tensor')
- new_hidden_square: float32 [2, 512, 36864], P(None, 'dp', 'tensor')
- loss_value: float32 [], replicated
The draws below stay inside these ranges and needn't reach their ends.
All inputs are finite; a program needn't handle non-finite values.
Results may differ from the reference program's by a relative error of at most 0.0059.
Values may be sent and summed in bfloat16 or wider, within the bound.
A program may use at most 128 MiB of HBM per device.

```python
import math
import jax
import jax.numpy as jnp
from jax import lax

D = 18432
FF = 36864
R = 512
TOK_DEV = 384
TOKENS = 6144
N_DP = 16


def draw_target(key, part):
    key = jax.random.fold_in(key, 7)
    key_column, key_noise = jax.random.split(key, 2)
    column = 0.75 * jnp.clip(jax.random.normal(key_column, (1, D), jnp.float32), -3.0, 3.0)
    noise = jnp.clip(jax.random.normal(key_noise, (TOKENS, D), jnp.float32), -3.0, 3.0)
    return jnp.clip(column + noise, -6.0, 6.0).astype(jnp.bfloat16)


def block_scale(stream_key, shape, cuts, smallest, high):
    def one(dim, shards_of):
        heights = jax.random.uniform(jax.random.fold_in(jax.random.fold_in(stream_key, 6), dim), (shards_of,), jnp.float32, smallest / len(cuts), high / len(cuts))
        return jnp.repeat(jnp.exp(heights), shape[dim] // shards_of).reshape((-1,) + (1,) * (len(shape) - dim - 1))

    level = one(*cuts[0])
    for cut in cuts[1:]:
        level = level * one(*cut)
    return level


def bell_draw(rng, extent, deviation, limit, cuts=(), dtype=jnp.bfloat16):
    values = deviation * jax.random.normal(rng, extent, jnp.float32)
    if cuts:
        values = values * block_scale(rng, extent, cuts, -0.22, 0.18)
    return jnp.clip(values, -limit, limit).astype(dtype)


def setup_inputs(seed: int = 0) -> dict:
    key_of = jax.random.split(jax.random.key(seed), 11)
    tokens = bell_draw(key_of[0], (TOKENS, D), 1.0, 6.0, ((0, 16), (1, 16)))
    target = draw_target(jax.random.fold_in(key_of[10], 71), 0)
    first_in = bell_draw(key_of[2], (R, D), D ** -0.5, 0.046875, ((0, 16), (1, 16)), jnp.float32)
    first_out = bell_draw(key_of[3], (R, FF), R ** -0.5, 0.25, ((0, 16), (1, 16)), jnp.float32)
    second_in = bell_draw(key_of[4], (R, FF), FF ** -0.5, 0.03125, ((0, 16), (1, 16)), jnp.float32)
    second_out = bell_draw(key_of[5], (R, D), R ** -0.5, 0.25, ((0, 16), (1, 16)), jnp.float32)
    width_mean = bell_draw(key_of[6], (2, R, D), (0.15 / (2 * R * (D + FF)) ** 0.5), 0.00030517578, ((1, 16), (2, 16)), jnp.float32)
    width_square = jnp.clip(jnp.exp(math.log(1.7660635620586618e-08) - 4.6051702 * jax.random.uniform(key_of[7], (2, R, D), jnp.float32) ** block_scale(key_of[7], (2, R, D), ((1, 16), (2, 16)), -0.2, 0.2)), 1.7660635454053164e-10, 1.7660635620586618e-08)
    hidden_mean = bell_draw(key_of[8], (2, R, FF), (0.15 / (2 * R * (D + FF)) ** 0.5), 0.00030517578, ((1, 16), (2, 16)), jnp.float32)
    hidden_square = jnp.clip(jnp.exp(math.log(1.7660635620586618e-08) - 4.6051702 * jax.random.uniform(key_of[9], (2, R, FF), jnp.float32) ** block_scale(key_of[9], (2, R, FF), ((1, 16), (2, 16)), -0.2, 0.2)), 1.7660635454053164e-10, 1.7660635620586618e-08)
    return dict(tokens=tokens, target=target, first_in=first_in, first_out=first_out, second_in=second_in, second_out=second_out, width_mean=width_mean, width_square=width_square, hidden_mean=hidden_mean, hidden_square=hidden_square)


beta_one = 0.9
beta_two = 0.95
learn_rate = 0.1
tiny_eps = 1e-08

def adam_update(param, grad, mean, square):
    new_mean = beta_one * mean + (1.0 - beta_one) * grad
    new_square = beta_two * square + (1.0 - beta_two) * grad * grad
    corrected = new_mean / (1.0 - beta_one ** 10)
    spread = jnp.sqrt(new_square / (1.0 - beta_two ** 10)) + tiny_eps
    return (param - learn_rate * corrected / spread, new_mean, new_square)

def reference(tokens, target, first_in, first_out, second_in, second_out, width_mean, width_square, hidden_mean, hidden_square):
    copy_pi = first_in.astype(jnp.bfloat16)
    copy_po = first_out.astype(jnp.bfloat16)
    copy_qi = second_in.astype(jnp.bfloat16)
    copy_qo = second_out.astype(jnp.bfloat16)
    tok_blocks = tokens.reshape(N_DP, TOK_DEV, D)
    tgt_blocks = target.reshape(N_DP, TOK_DEV, D)

    def one_block(totals, pieces):
        block_tokens, block_target = pieces
        rank_in = jnp.dot(block_tokens, copy_pi.T, preferred_element_type=jnp.float32).astype(jnp.bfloat16)
        pre = jnp.dot(rank_in, copy_po, preferred_element_type=jnp.float32)
        hidden = jnp.square(jnp.maximum(pre, 0.0)).astype(jnp.bfloat16)
        rank_out = jnp.dot(hidden, copy_qi.T, preferred_element_type=jnp.float32).astype(jnp.bfloat16)
        misfit = jnp.dot(rank_out, copy_qo, preferred_element_type=jnp.float32) - block_target.astype(jnp.float32)
        grad_out = (misfit / TOKENS).astype(jnp.bfloat16)
        grad_rank_out = jnp.dot(grad_out, copy_qo.T, preferred_element_type=jnp.float32).astype(jnp.bfloat16)
        grad_pre = (jnp.dot(grad_rank_out, copy_qi, preferred_element_type=jnp.float32) * 2.0 * jnp.maximum(pre, 0.0)).astype(jnp.bfloat16)
        grad_rank_in = jnp.dot(grad_pre, copy_po.T, preferred_element_type=jnp.float32).astype(jnp.bfloat16)
        grad_pi = jnp.dot(grad_rank_in.T, block_tokens, preferred_element_type=jnp.float32)
        grad_qo = jnp.dot(rank_out.T, grad_out, preferred_element_type=jnp.float32)
        grad_po = jnp.dot(rank_in.T, grad_pre, preferred_element_type=jnp.float32)
        grad_qi = jnp.dot(grad_rank_out.T, hidden, preferred_element_type=jnp.float32)
        loss_acc, acc_pi, acc_po, acc_qi, acc_qo = totals
        return ((loss_acc + jnp.sum(misfit * misfit), acc_pi + grad_pi, acc_po + grad_po, acc_qi + grad_qi, acc_qo + grad_qo), None)
    start_totals = (jnp.zeros((), jnp.float32), jnp.zeros((R, D), jnp.float32), jnp.zeros((R, FF), jnp.float32), jnp.zeros((R, FF), jnp.float32), jnp.zeros((R, D), jnp.float32))
    totals, unused = lax.scan(one_block, start_totals, (tok_blocks, tgt_blocks))
    loss_acc, grad_pi, grad_po, grad_qi, grad_qo = totals
    squares = jnp.sum(grad_pi * grad_pi) + jnp.sum(grad_po * grad_po) + jnp.sum(grad_qi * grad_qi) + jnp.sum(grad_qo * grad_qo)
    scale = 1.0 / jnp.maximum(jnp.sqrt(squares), 1.0)
    new_pi, mean_pi, square_pi = adam_update(first_in, grad_pi * scale, width_mean[0], width_square[0])
    new_qo, mean_qo, square_qo = adam_update(second_out, grad_qo * scale, width_mean[1], width_square[1])
    new_po, mean_po, square_po = adam_update(first_out, grad_po * scale, hidden_mean[0], hidden_square[0])
    new_qi, mean_qi, square_qi = adam_update(second_in, grad_qi * scale, hidden_mean[1], hidden_square[1])
    loss_value = loss_acc / (2.0 * TOKENS)
    return (new_pi, new_po, new_qi, new_qo, jnp.stack([mean_pi, mean_qo]), jnp.stack([square_pi, square_qo]), jnp.stack([mean_po, mean_qi]), jnp.stack([square_po, square_qi]), loss_value)
```

```python
import functools

import jax
import jax.numpy as jnp
from jax import lax
from jax.experimental import pallas as pl
from jax.experimental.pallas import tpu as pltpu
from jax.sharding import PartitionSpec as P

beta_one = 0.9
beta_two = 0.95
learn_rate = 0.1
tiny_eps = 1e-08

MESH = pl.DeviceIdType.MESH
BF = jnp.bfloat16
F32 = jnp.float32

NX, NY, NZ = 4, 4, 8
DP = NX * NY
TP = NZ * 2
ROWS = 32
RANK = DP * ROWS
TOKD = 384
HALF = TOKD // 2
TOTAL = TOKD * DP
PI, PO, QI, QO = 0, 1, 2, 3


def dot_nt(left, right):
    return lax.dot_general(
        left, right, (((1,), (1,)), ((), ())), preferred_element_type=F32
    )


def dot_nn(left, right):
    return jnp.dot(left, right, preferred_element_type=F32)


def body(
    tokens, target, fi, fo, si, so,
    g_pi, g_po, g_qi, g_qo, stat,
    tok, tgt, wf0, wf1, wf2, wf3,
    w0, w1, w2, w3, gr0, gr1, gr2, gr3,
    ra0, ra1, ra2, ra3, rb0, rb1, rb2, rb3, rc0, rc1, rc2, rc3,
    rank, ranks_t, relu, hid, gpre, gout, partial,
    sib_send, sib_recv, z_keep, z_send, z_recv, loss_acc, sc_buf,
    ld_sem, ag_send, ag_recv, rs_send, rs_recv, ar_send, ar_recv, sc_send, sc_recv,
):
    me_dp = lax.axis_index("dp")
    me_t = lax.axis_index("tensor")
    x, y = me_dp // NY, lax.rem(me_dp, NY)
    z, c = me_t // 2, lax.rem(me_t, 2)
    wf = (wf0, wf1, wf2, wf3)
    w = (w0, w1, w2, w3)
    gr = (gr0, gr1, gr2, gr3)
    ra = (ra0, ra1, ra2, ra3)
    rb = (rb0, rb1, rb2, rb3)
    rc = (rc0, rc1, rc2, rc3)
    gouts = (g_pi, g_po, g_qi, g_qo)
    cols = tuple(r.shape[-1] for r in wf)

    def at_x(d):
        return (lax.rem(x + d, NX) * NY + y, me_t)

    def at_y(d):
        return (x * NY + lax.rem(y + d, NY), me_t)

    def at_z(d):
        return (me_dp, lax.rem(z + d, NZ) * 2 + c)

    sibling = (me_dp, z * 2 + 1 - c)

    def send(src, dst, s_sem, r_sem, where):
        pltpu.make_async_remote_copy(
            src_ref=src, dst_ref=dst, send_sem=s_sem, recv_sem=r_sem,
            device_id=where, device_id_type=MESH,
        ).start()

    def wait_for(ref, sem):
        pltpu.make_async_copy(ref, ref, sem).wait()

    loads = [
        pltpu.make_async_copy(s, d, ld_sem.at[k])
        for k, (s, d) in enumerate(
            ((fi, wf0), (fo, wf1), (tokens, tok), (si, wf2), (so, wf3), (target, tgt))
        )
    ]
    for cp in loads:
        cp.start()

    barrier = pltpu.get_barrier_semaphore()

    def greet(k, carry):
        pl.semaphore_signal(
            barrier, inc=1, device_id=(lax.rem(me_dp + k, DP), me_t), device_id_type=MESH
        )
        pl.semaphore_signal(
            barrier, inc=1, device_id=(me_dp, lax.rem(me_t + k, TP)), device_id_type=MESH
        )
        return carry

    lax.fori_loop(1, DP, greet, 0)

    def cast(a):
        w[a][x, y] = wf[a][...].astype(BF).reshape(2, 16, cols[a])

    def gather_one(a):
        for d in (2, 1, 3):
            own = w[a].at[x, y, 0]
            send(own, own, ag_send.at[a, 0, 0], ag_recv.at[a, 0, 0], at_x(d))
            own = w[a].at[x, y, 1]
            send(own, own, ag_send.at[a, 0, 1], ag_recv.at[a, 0, 1], at_y(d))

    def gather_two(a):
        wait_for(w[a].at[pl.ds(0, 3), 0, 0], ag_recv.at[a, 0, 0])
        for d in (2, 1, 3):
            part = w[a].at[:, y, 0]
            send(part, part, ag_send.at[a, 1, 0], ag_recv.at[a, 1, 0], at_y(d))
        wait_for(w[a].at[0, pl.ds(0, 3), 1], ag_recv.at[a, 0, 1])
        for d in (2, 1, 3):
            part = w[a].at[x, :, 1]
            send(part, part, ag_send.at[a, 1, 1], ag_recv.at[a, 1, 1], at_x(d))

    def gather_end(a):
        wait_for(w[a].at[:, pl.ds(0, 3), 0], ag_recv.at[a, 1, 0])
        wait_for(w[a].at[pl.ds(0, 3), :, 1], ag_recv.at[a, 1, 1])

    def sum_send(s, h, left, a):
        n = 1 - c
        sib_send[s, h] = dot_nt(left, w[a][pl.ds(2 * n, 2)].reshape(256, cols[a])).astype(BF)
        send(sib_send.at[s, h], sib_recv.at[s, h], ar_send.at[s, h, 0], ar_recv.at[s, h, 0], sibling)
        partial[h] = dot_nt(left, w[a][pl.ds(2 * c, 2)].reshape(256, cols[a]))

    def sum_scatter(s, h):
        wait_for(sib_recv.at[s, h], ar_recv.at[s, h, 0])
        both = partial[h] + sib_recv[s, h].astype(F32)
        for k in range(NZ):
            zr, zc = k // 2, k % 2
            piece = both[zr * 48 : (zr + 1) * 48, zc * 128 : (zc + 1) * 128]
            z_keep[h, k] = piece
            z_send[s, h, k] = piece.astype(BF)

        def one(i, carry):
            d = lax.rem(i + 3, NZ - 1) + 1
            send(
                z_send.at[s, h, lax.rem(z + d, NZ)], z_recv.at[s, h, d - 1],
                ar_send.at[s, h, 1], ar_recv.at[s, h, 1], at_z(d),
            )
            return carry

        lax.fori_loop(0, NZ - 1, one, 0)

    def spot(s, h):
        row = pl.multiple_of(h * HALF + (z // 2) * 48, 16)
        col = pl.multiple_of(c * 256 + lax.rem(z, 2) * 128, 128)
        return rank.at[s, pl.ds(row, 48), pl.ds(col, 128)]

    def sum_gather(s, h):
        wait_for(z_recv.at[s, h], ar_recv.at[s, h, 1])
        total = z_keep[h, z]
        for k in range(NZ - 1):
            total = total + z_recv[s, h, k].astype(F32)
        mine = spot(s, h)
        mine[...] = total.astype(BF)

        def one(i, carry):
            d = lax.rem(i + 3, NZ - 1) + 1
            send(mine, mine, ar_send.at[s, h, 2], ar_recv.at[s, h, 2], at_z(d))
            return carry

        lax.fori_loop(0, NZ - 1, one, 0)

    def half_of(s, h):
        col = pl.multiple_of(c * 256, 128)
        return rank.at[s, pl.ds(h * HALF, HALF), pl.ds(col, 256)]

    def sum_share(s, h):
        wait_for(z_recv.at[s, h], ar_recv.at[s, h, 2])
        part = half_of(s, h)
        send(part, part, ar_send.at[s, h, 3], ar_recv.at[s, h, 3], sibling)

    def sum_end(s, h):
        wait_for(half_of(s, h), ar_recv.at[s, h, 3])

    def scatter_one(a):
        for d in (2, 1, 3):
            send(
                gr[a].at[:, lax.rem(y + d, NY), 0], ra[a].at[0, d - 1],
                rs_send.at[a, 0, 0], rs_recv.at[a, 0, 0], at_y(d),
            )
            send(
                gr[a].at[lax.rem(x + d, NX), :, 1], ra[a].at[1, d - 1],
                rs_send.at[a, 0, 1], rs_recv.at[a, 0, 1], at_x(d),
            )

    def scatter_two(a):
        for half in range(2):
            wait_for(ra[a].at[half], rs_recv.at[a, 0, half])

            def one(k, carry):
                own = gr[a][k, y, 0] if half == 0 else gr[a][x, k, 1]
                total = own.astype(F32)
                for j in range(3):
                    total = total + ra[a][half, j, k].astype(F32)
                rb[a][half, k] = total.astype(BF)
                return carry

            lax.fori_loop(0, 4, one, 0)
            for d in (2, 1, 3):
                if half == 0:
                    there, where = lax.rem(x + d, NX), at_x(d)
                else:
                    there, where = lax.rem(y + d, NY), at_y(d)
                send(
                    rb[a].at[half, there], rc[a].at[half, d - 1],
                    rs_send.at[a, 1, half], rs_recv.at[a, 1, half], where,
                )

    def scatter_end(a):
        squares = jnp.zeros((8, 128), F32)
        for half in range(2):
            wait_for(rc[a].at[half], rs_recv.at[a, 1, half])
            total = rb[a][half, x if half == 0 else y].astype(F32)
            for j in range(3):
                total = total + rc[a][half, j].astype(F32)
            gouts[a][half * 16 : (half + 1) * 16, :] = total
            sq = total * total
            sq = sq[0:8] + sq[8:16]
            for j in range(cols[a] // 128):
                squares = squares + sq[:, j * 128 : (j + 1) * 128]
        return squares

    def gradient(a, s, right):
        ranks_t[...] = rank[s].T
        step = 256 if cols[a] % 256 == 0 else 384

        def one(j, carry):
            at = pl.ds(pl.multiple_of(j * step, 128), step)
            tile = dot_nn(ranks_t[...], right[:, at]).astype(BF)
            gr[a][:, :, :, :, at] = tile.reshape(NX, NY, 2, 16, step)
            return carry

        lax.fori_loop(0, cols[a] // step, one, 0)

    def tile_of(a, at, n):
        return w[a][:, :, :, :, at].reshape(RANK, n)

    def rows_of(h):
        return pl.ds(h * HALF, HALF)

    def stage_zero(h):
        sum_send(0, h, tok[rows_of(h), :], PI)

    def stage_one(h):
        left = rank[0, rows_of(h), :]

        def one(j, carry):
            at = pl.ds(pl.multiple_of(j * 256, 128), 256)
            pre = jnp.maximum(dot_nn(left, tile_of(PO, at, 256)), 0.0)
            relu[rows_of(h), at] = pre
            hid[rows_of(h), at] = (pre * pre).astype(BF)
            return carry

        lax.fori_loop(0, cols[PO] // 256, one, 0)

    def stage_two(h):
        left = rank[1, rows_of(h), :]

        def one(j, carry):
            at = pl.ds(pl.multiple_of(j * 384, 128), 384)
            misfit = dot_nn(left, tile_of(QO, at, 384)) - tgt[rows_of(h), at].astype(F32)
            gout[rows_of(h), at] = (misfit * (1.0 / TOTAL)).astype(BF)
            sq = (misfit * misfit).reshape(HALF // 8, 8, 384).sum(axis=0)
            loss_acc[...] += sq[:, 0:128] + sq[:, 128:256] + sq[:, 256:384]
            return carry

        lax.fori_loop(0, cols[QO] // 384, one, 0)

    def stage_three(h):
        left = rank[2, rows_of(h), :]

        def one(j, carry):
            at = pl.ds(pl.multiple_of(j * 256, 128), 256)
            up = dot_nn(left, tile_of(QI, at, 256))
            gpre[rows_of(h), at] = (up * 2.0 * relu[rows_of(h), at]).astype(BF)
            return carry

        lax.fori_loop(0, cols[QI] // 256, one, 0)

    loss_acc[...] = jnp.zeros_like(loss_acc)
    loads[0].wait()
    cast(PI)
    pl.semaphore_wait(barrier, 2 * (DP - 1))
    gather_one(PI)
    loads[1].wait()
    cast(PO)
    gather_one(PO)
    loads[3].wait()
    cast(QI)
    loads[4].wait()
    cast(QO)
    gather_two(PI)
    gather_two(PO)
    gather_one(QI)
    gather_one(QO)
    loads[2].wait()
    loads[5].wait()
    gather_end(PI)
    stage_zero(0)
    stage_zero(1)
    sum_scatter(0, 0)
    sum_scatter(0, 1)
    gather_two(QI)
    sum_gather(0, 0)
    sum_gather(0, 1)
    gather_two(QO)
    sum_share(0, 0)
    sum_share(0, 1)
    gather_end(PO)
    sum_end(0, 0)
    stage_one(0)
    gather_end(QI)
    sum_send(1, 0, hid[rows_of(0), :], QI)
    sum_end(0, 1)
    stage_one(1)
    sum_send(1, 1, hid[rows_of(1), :], QI)
    sum_scatter(1, 0)
    sum_scatter(1, 1)
    sum_gather(1, 0)
    sum_gather(1, 1)
    sum_share(1, 0)
    sum_share(1, 1)
    gather_end(QO)
    sum_end(1, 0)
    stage_two(0)
    sum_send(2, 0, gout[rows_of(0), :], QO)
    sum_end(1, 1)
    stage_two(1)
    sum_send(2, 1, gout[rows_of(1), :], QO)
    sum_scatter(2, 0)
    sum_scatter(2, 1)
    gradient(QO, 1, gout)
    scatter_one(QO)
    sum_gather(2, 0)
    sum_gather(2, 1)
    sum_share(2, 0)
    sum_share(2, 1)
    sum_end(2, 0)
    sum_end(2, 1)
    gradient(QI, 2, hid)
    scatter_one(QI)
    stage_three(0)
    sum_send(3, 0, gpre[rows_of(0), :], PO)
    stage_three(1)
    sum_send(3, 1, gpre[rows_of(1), :], PO)
    sum_scatter(3, 0)
    sum_scatter(3, 1)
    gradient(PO, 0, gpre)
    scatter_one(PO)
    sum_gather(3, 0)
    sum_gather(3, 1)
    scatter_two(QO)
    sum_share(3, 0)
    sum_share(3, 1)
    sum_end(3, 0)
    sum_end(3, 1)
    gradient(PI, 3, tok)
    scatter_one(PI)
    scatter_two(QI)
    scatter_two(PO)
    scatter_two(PI)
    squares = scatter_end(QO)
    squares = squares + scatter_end(QI)
    squares = squares + scatter_end(PO)
    squares = squares + scatter_end(PI)

    sc_buf[0, me_t, 0] = squares
    sc_buf[0, me_t, 1] = loss_acc[...]

    def over_tensor(k, carry):
        own = sc_buf.at[0, me_t]
        send(own, own, sc_send.at[0], sc_recv.at[0], (me_dp, lax.rem(me_t + k, TP)))
        return carry

    lax.fori_loop(1, TP, over_tensor, 0)
    wait_for(sc_buf.at[0, pl.ds(0, TP - 1)], sc_recv.at[0])
    sc_buf[1, me_dp] = jnp.sum(sc_buf[0], axis=0)

    def over_dp(k, carry):
        own = sc_buf.at[1, me_dp]
        send(own, own, sc_send.at[1], sc_recv.at[1], (lax.rem(me_dp + k, DP), me_t))
        return carry

    lax.fori_loop(1, DP, over_dp, 0)
    wait_for(sc_buf.at[1, pl.ds(0, DP - 1)], sc_recv.at[1])
    stat[...] = jnp.sum(sc_buf[1], axis=0)

    for a in range(4):
        for half in range(2):
            wait_for(w[a].at[pl.ds(0, 3), 0, 0], ag_send.at[a, 0, half])
            wait_for(w[a].at[:, pl.ds(0, 3), 0], ag_send.at[a, 1, half])
            wait_for(ra[a].at[half], rs_send.at[a, 0, half])
            wait_for(rc[a].at[half], rs_send.at[a, 1, half])
    for s in range(4):
        for h in range(2):
            wait_for(sib_recv.at[s, h], ar_send.at[s, h, 0])
            wait_for(z_recv.at[s, h], ar_send.at[s, h, 1])
            wait_for(z_recv.at[s, h], ar_send.at[s, h, 2])
            wait_for(sib_recv.at[s, h], ar_send.at[s, h, 3])
    for k in range(2):
        wait_for(sc_buf.at[k, pl.ds(0, TP - 1)], sc_send.at[k])


def adam_body(
    stat, g_pi, g_po, g_qi, g_qo, p_pi, p_po, p_qi, p_qo, wm, ws, hm, hs,
    n_pi, n_po, n_qi, n_qo, nwm, nws, nhm, nhs, loss,
):
    squares = jnp.sum(stat[0])
    scale = 1.0 / jnp.maximum(jnp.sqrt(squares), 1.0)
    loss[0, 0] = jnp.sum(stat[1]) / (2.0 * TOTAL)
    for g, p, m, v, k, new_p, new_m, new_v in (
        (g_pi, p_pi, wm, ws, 0, n_pi, nwm, nws),
        (g_qo, p_qo, wm, ws, 1, n_qo, nwm, nws),
        (g_po, p_po, hm, hs, 0, n_po, nhm, nhs),
        (g_qi, p_qi, hm, hs, 1, n_qi, nhm, nhs),
    ):
        grad = g[...] * scale
        mean = beta_one * m[k] + (1.0 - beta_one) * grad
        square = beta_two * v[k] + (1.0 - beta_two) * grad * grad
        corrected = mean * (1.0 / (1.0 - beta_one**10))
        spread = jnp.sqrt(square * (1.0 / (1.0 - beta_two**10))) + tiny_eps
        new_p[...] = p[...] - learn_rate * corrected / spread
        new_m[k] = mean
        new_v[k] = square


def shards(
    tokens, target, first_in, first_out, second_in, second_out,
    width_mean, width_square, hidden_mean, hidden_square,
):
    wide = first_in.shape[1]
    deep = first_out.shape[1]
    cols = (wide, deep, deep, wide)
    vm = pltpu.VMEM
    dma = pltpu.SemaphoreType.DMA
    scratch = [vm((TOKD, wide), BF), vm((TOKD, wide), BF)]
    scratch += [vm((ROWS, n), F32) for n in cols]
    scratch += [vm((NX, NY, 2, 16, n), BF) for n in cols]
    scratch += [vm((NX, NY, 2, 16, n), BF) for n in cols]
    scratch += [vm((2, 3, 4, 16, n), BF) for n in cols]
    scratch += [vm((2, 4, 16, n), BF) for n in cols]
    scratch += [vm((2, 3, 16, n), BF) for n in cols]
    scratch += [
        vm((4, TOKD, RANK), BF),
        vm((RANK, TOKD), BF),
        vm((TOKD, deep), F32),
        vm((TOKD, deep), BF),
        vm((TOKD, deep), BF),
        vm((TOKD, wide), BF),
        vm((2, HALF, 256), F32),
        vm((4, 2, HALF, 256), BF),
        vm((4, 2, HALF, 256), BF),
        vm((2, NZ, 48, 128), F32),
        vm((4, 2, NZ, 48, 128), BF),
        vm((4, 2, NZ - 1, 48, 128), BF),
        vm((8, 128), F32),
        vm((2, 16, 2, 8, 128), F32),
        dma((6,)),
        dma((4, 2, 2)), dma((4, 2, 2)),
        dma((4, 2, 2)), dma((4, 2, 2)),
        dma((4, 2, 4)), dma((4, 2, 4)),
        dma((2,)), dma((2,)),
    ]
    whole = pl.BlockSpec(memory_space=pltpu.VMEM)
    g_pi, g_po, g_qi, g_qo, stat = pl.pallas_call(
        body,
        name="step",
        out_shape=[jax.ShapeDtypeStruct((ROWS, n), F32) for n in cols]
        + [jax.ShapeDtypeStruct((2, 8, 128), F32)],
        in_specs=[pl.BlockSpec(memory_space=pl.ANY)] * 6,
        out_specs=[whole] * 5,
        scratch_shapes=scratch,
        compiler_params=pltpu.CompilerParams(
            collective_id=0, has_side_effects=True, vmem_limit_bytes=58 * 2**20
        ),
    )(tokens, target, first_in, first_out, second_in, second_out)

    steps = 3
    w2 = pl.BlockSpec((ROWS, wide // steps), lambda i: (0, i))
    h2 = pl.BlockSpec((ROWS, deep // steps), lambda i: (0, i))
    w3 = pl.BlockSpec((2, ROWS, wide // steps), lambda i: (0, 0, i))
    h3 = pl.BlockSpec((2, ROWS, deep // steps), lambda i: (0, 0, i))
    outs = pl.pallas_call(
        adam_body,
        name="adam",
        grid=(steps,),
        out_shape=[jax.ShapeDtypeStruct((ROWS, n), F32) for n in cols]
        + [jax.ShapeDtypeStruct((2, ROWS, n), F32) for n in (wide, wide, deep, deep)]
        + [jax.ShapeDtypeStruct((1, 1), F32)],
        in_specs=[
            pl.BlockSpec((2, 8, 128), lambda i: (0, 0, 0)),
            w2, h2, h2, w2, w2, h2, h2, w2, w3, w3, h3, h3,
        ],
        out_specs=[
            w2, h2, h2, w2, w3, w3, h3, h3,
            pl.BlockSpec((1, 1), lambda i: (0, 0), memory_space=pltpu.SMEM),
        ],
        compiler_params=pltpu.CompilerParams(vmem_limit_bytes=40 * 2**20),
    )(
        stat, g_pi, g_po, g_qi, g_qo, first_in, first_out, second_in, second_out,
        width_mean, width_square, hidden_mean, hidden_square,
    )
    return tuple(outs[:8]) + (outs[8].reshape(()),)


def solution(mesh):
    two = P("dp", "tensor")
    three = P(None, "dp", "tensor")
    return jax.shard_map(
        shards,
        mesh=mesh,
        in_specs=(two,) * 6 + (three,) * 4,
        out_specs=(two,) * 4 + (three,) * 4 + (P(),),
        check_vma=False,
    )
```

```python
import functools

import jax
import jax.numpy as jnp
from jax import lax
from jax.experimental import pallas as pl
from jax.experimental.pallas import tpu as pltpu
from jax.sharding import PartitionSpec as P

beta_one = 0.9
beta_two = 0.95
learn_rate = 0.1
tiny_eps = 1e-08

MESH = pl.DeviceIdType.MESH
BF = jnp.bfloat16
F32 = jnp.float32

NX, NY, NZ = 4, 4, 8
DP = NX * NY
TP = NZ * 2
ROWS = 32
RANK = DP * ROWS
TOKD = 384
HALF = TOKD // 2
TOTAL = TOKD * DP
PI, PO, QI, QO = 0, 1, 2, 3
GRAM = 4


def dot_nt(left, right):
    return lax.dot_general(
        left, right, (((1,), (1,)), ((), ())), preferred_element_type=F32
    )


def dot_nn(left, right):
    return jnp.dot(left, right, preferred_element_type=F32)


def body(
    tokens, target, fi, fo, si, so,
    g_pi, g_po, g_qi, g_qo, stat,
    tok, tgt, wf0, wf1, wf2, wf3,
    w0, w1, w2, w3, gr0, gr1, gr2, gr3,
    ra0, ra1, ra2, ra3, rb0, rb1, rb2, rb3, rc0, rc1, rc2, rc3,
    cb0, cb1, cb2, cb3,
    rank, back, ranks_t, relu, hid, gpre, gout, partial,
    sib_send, sib_recv, z_keep, z_send, z_recv,
    gram, gpartial, gsib_send, gsib_recv, gz_keep, gz_send, gz_recv, loss_acc, sc_buf,
    ld_sem, ag_send, ag_recv, rs_send, rs_recv, ar_send, ar_recv, sc_send, sc_recv,
):
    me_dp = lax.axis_index("dp")
    me_t = lax.axis_index("tensor")
    x, y = me_dp // NY, lax.rem(me_dp, NY)
    z, c = me_t // 2, lax.rem(me_t, 2)
    wf = (wf0, wf1, wf2, wf3)
    w = (w0, w1, w2, w3)
    gr = (gr0, gr1, gr2, gr3)
    ra = (ra0, ra1, ra2, ra3)
    rb = (rb0, rb1, rb2, rb3)
    rc = (rc0, rc1, rc2, rc3)
    cb = (cb0, cb1, cb2, cb3)
    gouts = (g_pi, g_po, g_qi, g_qo)
    cols = tuple(r.shape[-1] for r in wf)

    def at_x(d):
        return (lax.rem(x + d, NX) * NY + y, me_t)

    def at_y(d):
        return (x * NY + lax.rem(y + d, NY), me_t)

    def at_z(d):
        return (me_dp, lax.rem(z + d, NZ) * 2 + c)

    sibling = (me_dp, z * 2 + 1 - c)

    sent = []

    def start(src, dst, s_sem, r_sem, where):
        pltpu.make_async_remote_copy(
            src_ref=src, dst_ref=dst, send_sem=s_sem, recv_sem=r_sem,
            device_id=where, device_id_type=MESH,
        ).start()

    def send(src, dst, sems, spot_of, where):
        start(src, dst, sems[0].at[spot_of], sems[1].at[spot_of], where)
        sent.append((src, sems[0], spot_of))

    def wait_for(ref, sem, spot_of):
        at = sem.at[spot_of]
        pltpu.make_async_copy(ref, ref, at).wait()

    ag = (ag_send, ag_recv)
    rs = (rs_send, rs_recv)
    ar = (ar_send, ar_recv)
    low, high = pl.ds(0, 2), pl.ds(2, 2)

    def around(m):
        return lax.rem(m + 1, 4), lax.rem(m + 2, 4), lax.rem(m + 3, 4)

    loads = [
        pltpu.make_async_copy(s, d, ld_sem.at[k])
        for k, (s, d) in enumerate(
            ((fi, wf0), (fo, wf1), (tokens, tok), (si, wf2), (so, wf3), (target, tgt))
        )
    ]
    for cp in loads:
        cp.start()

    barrier = pltpu.get_barrier_semaphore()

    def greet(k, carry):
        pl.semaphore_signal(
            barrier, inc=1, device_id=(lax.rem(me_dp + k, DP), me_t), device_id_type=MESH
        )
        pl.semaphore_signal(
            barrier, inc=1, device_id=(me_dp, lax.rem(me_t + k, TP)), device_id_type=MESH
        )
        return carry

    lax.fori_loop(1, DP, greet, 0)

    def cast(a):
        w[a][x, y] = wf[a][...].astype(BF).reshape(2, 16, cols[a])

    def slot(a, half, p, q, part=slice(None)):
        if half == 0:
            return w[a].at[p, q, 0, :, part]
        return w[a].at[q, p, 1, :, part]

    def places(half):
        return (x, y, at_x, at_y) if half == 0 else (y, x, at_y, at_x)

    def gather_one(a):
        for half in range(2):
            m, q, go, _ = places(half)
            own = slot(a, half, m, q)
            for d in (2, 1, 3):
                send(own, own, ag, (a, 0, half, d - 1), go(d))

    def gather_two(a):
        for half in range(2):
            m, q, _, go = places(half)
            for d in range(3):
                wait_for(slot(a, half, m, q), ag_recv, (a, 0, half, d))
            row = slot(a, half, pl.ds(0, 4), q)
            send(row, row, ag, (a, 1, half, 0), go(1))
            send(row, row, ag, (a, 1, half, 1), go(3))

    def gather_last(a):
        for half in range(2):
            _, q, _, go = places(half)
            right, _, left = around(q)
            wait_for(slot(a, half, pl.ds(0, 4), left), ag_recv, (a, 1, half, 0))
            part = slot(a, half, low, left)
            send(part, part, ag, (a, 2, half, 0), go(1))
            wait_for(slot(a, half, pl.ds(0, 4), right), ag_recv, (a, 1, half, 1))
            part = slot(a, half, high, right)
            send(part, part, ag, (a, 2, half, 1), go(3))

    def gather_end(a):
        for half in range(2):
            _, q, _, _ = places(half)
            _, far, _ = around(q)
            wait_for(slot(a, half, low, far), ag_recv, (a, 2, half, 0))
            wait_for(slot(a, half, high, far), ag_recv, (a, 2, half, 1))

    def set_of(s):
        if s == GRAM:
            return gsib_send, gsib_recv, gz_keep, gz_send, gz_recv, gram, gpartial
        return (
            sib_send.at[s], sib_recv.at[s], z_keep.at[s], z_send.at[s], z_recv.at[s], rank.at[s], partial,
        )

    def sum_send(s, h, left, a):
        out, into, _, _, _, _, keep = set_of(s)
        n = 1 - c
        out[h] = dot_nt(left, w[a][pl.ds(2 * n, 2)].reshape(256, cols[a])).astype(BF)
        send(out.at[h], into.at[h], ar, (s, h, 0), sibling)
        keep[h] = dot_nt(left, w[a][pl.ds(2 * c, 2)].reshape(256, cols[a]))

    def sum_scatter(s, h):
        _, into, own, out, there, _, keep = set_of(s)
        tall = out.shape[2]
        wait_for(into.at[h], ar_recv, (s, h, 0))
        both = keep[h] + into[h].astype(F32)
        for k in range(NZ):
            zr, zc = k // 2, k % 2
            piece = both[zr * tall : (zr + 1) * tall, zc * 128 : (zc + 1) * 128]
            own[h, k] = piece
            out[h, k] = piece.astype(BF)

        def one(i, carry):
            d = lax.rem(i + 3, NZ - 1) + 1
            start(
                out.at[h, lax.rem(z + d, NZ)], there.at[h, d - 1],
                ar_send.at[s, h, 1], ar_recv.at[s, h, 1], at_z(d),
            )
            return carry

        lax.fori_loop(0, NZ - 1, one, 0)
        sent.append((there.at[h], ar_send, (s, h, 1)))

    def sum_gather(s, h):
        _, _, own, _, there, result, _ = set_of(s)
        tall = own.shape[2]
        wait_for(there.at[h], ar_recv, (s, h, 1))
        total = own[h, z]
        for k in range(NZ - 1):
            total = total + there[h, k].astype(F32)
        row = pl.multiple_of(h * 4 * tall + (z // 2) * tall, 16)
        col = pl.multiple_of(c * 256 + lax.rem(z, 2) * 128, 128)
        mine = result.at[pl.ds(row, tall), pl.ds(col, 128)]
        mine[...] = total.astype(BF)

        def one(i, carry):
            d = lax.rem(i + 3, NZ - 1) + 1
            start(mine, mine, ar_send.at[s, h, 2], ar_recv.at[s, h, 2], at_z(d))
            return carry

        lax.fori_loop(0, NZ - 1, one, 0)
        sent.append((there.at[h], ar_send, (s, h, 2)))

    def half_of(s, h):
        _, _, own, _, _, result, _ = set_of(s)
        tall = own.shape[2]
        col = pl.multiple_of(c * 256, 128)
        return result.at[pl.ds(h * 4 * tall, 4 * tall), pl.ds(col, 256)]

    def sum_share(s, h):
        there = set_of(s)[4]
        wait_for(there.at[h], ar_recv, (s, h, 2))
        part = half_of(s, h)
        send(part, part, ar, (s, h, 3), sibling)

    def sum_end(s, h):
        wait_for(half_of(s, h), ar_recv, (s, h, 3))

    def piece(a, half, t, part):
        return gr[a].at[part, t, 0] if half == 0 else gr[a].at[t, part, 1]

    def add_blocks(out, first, terms, count):
        def one(k, carry):
            total = first(k)[...].astype(F32)
            for term in terms:
                total = total + term(k)[...].astype(F32)
            out(k)[...] = total.astype(BF)
            return carry

        lax.fori_loop(0, count, one, 0)

    def scatter_one(a):
        for half in range(2):
            _, m, _, go = places(half)
            right, far, left = around(m)
            send(piece(a, half, far, low), ra[a].at[half, 0, low], rs, (a, 0, half, 0), go(1))
            send(piece(a, half, far, high), ra[a].at[half, 0, high], rs, (a, 0, half, 1), go(3))
            send(piece(a, half, right, high), ra[a].at[half, 1, high], rs, (a, 1, half, 0), go(1))
            send(piece(a, half, left, low), ra[a].at[half, 1, low], rs, (a, 1, half, 1), go(3))

    def scatter_mid(a):
        for half in range(2):
            _, m, _, go = places(half)
            right, _, left = around(m)
            for side, (part, base, to, d) in enumerate(((low, 0, right, 1), (high, 2, left, 3))):
                wait_for(ra[a].at[half, 0, part], rs_recv, (a, 0, half, side))
                add_blocks(
                    lambda k: cb[a].at[half, base + k],
                    lambda k: piece(a, half, to, base + k),
                    (lambda k: ra[a].at[half, 0, base + k],),
                    2,
                )
                send(cb[a].at[half, part], ra[a].at[half, 2, part], rs, (a, 2, half, side), go(d))

    def scatter_two(a):
        for half in range(2):
            q, m, go, _ = places(half)
            wait_for(ra[a].at[half, 1, high], rs_recv, (a, 1, half, 0))
            wait_for(ra[a].at[half, 1, low], rs_recv, (a, 1, half, 1))
            wait_for(ra[a].at[half, 2, low], rs_recv, (a, 2, half, 0))
            wait_for(ra[a].at[half, 2, high], rs_recv, (a, 2, half, 1))
            add_blocks(
                lambda k: rb[a].at[half, k],
                lambda k: piece(a, half, m, k),
                (lambda k: ra[a].at[half, 1, k], lambda k: ra[a].at[half, 2, k]),
                4,
            )
            for d in (2, 1, 3):
                send(
                    rb[a].at[half, lax.rem(q + d, 4)], rc[a].at[half, d - 1],
                    rs, (a, 3, half, d - 1), go(d),
                )

    def scatter_end(a):
        squares = jnp.zeros((8, 128), F32)
        for half in range(2):
            q, _, _, _ = places(half)
            total = rb[a][half, q].astype(F32)
            for d in range(3):
                wait_for(rc[a].at[half, d], rs_recv, (a, 3, half, d))
                total = total + rc[a][half, d].astype(F32)
            gouts[a][half * 16 : (half + 1) * 16, :] = total
            sq = total * total
            sq = sq[0:8] + sq[8:16]
            for j in range(cols[a] // 128):
                squares = squares + sq[:, j * 128 : (j + 1) * 128]
        return squares

    def gradient(a, left, right):
        ranks_t[...] = left[...].T
        step = 768 if cols[a] % 768 == 0 else 384

        def one(j, carry):
            at = pl.ds(pl.multiple_of(j * step, 128), step)
            tile = dot_nn(ranks_t[...], right[:, at]).astype(BF)
            gr[a][:, :, :, :, at] = tile.reshape(NX, NY, 2, 16, step)
            return carry

        lax.fori_loop(0, cols[a] // step, one, 0)

    def tile_of(a, at, n):
        return w[a][:, :, :, :, at].reshape(RANK, n)

    def rows_of(h):
        return pl.ds(h * HALF, HALF)

    def stage_zero(h):
        sum_send(0, h, tok[rows_of(h), :], PI)

    def stage_one(h):
        left = rank[0, rows_of(h), :]

        def one(j, carry):
            at = pl.ds(pl.multiple_of(j * 768, 128), 768)
            pre = jnp.maximum(dot_nn(left, tile_of(PO, at, 768)), 0.0)
            relu[rows_of(h), at] = pre
            hid[rows_of(h), at] = (pre * pre).astype(BF)
            return carry

        lax.fori_loop(0, cols[PO] // 768, one, 0)

    def stage_two(h):
        left = rank[1, rows_of(h), :]

        def one(j, carry):
            at = pl.ds(pl.multiple_of(j * 384, 128), 384)
            misfit = dot_nn(left, tile_of(QO, at, 384)) - tgt[rows_of(h), at].astype(F32)
            gout[rows_of(h), at] = (misfit * (1.0 / TOTAL)).astype(BF)
            sq = (misfit * misfit).reshape(HALF // 8, 8, 384).sum(axis=0)
            loss_acc[...] += sq[:, 0:128] + sq[:, 128:256] + sq[:, 256:384]
            return carry

        lax.fori_loop(0, cols[QO] // 384, one, 0)

    def stage_back(h):
        up = dot_nn(rank[1, rows_of(h), :], gram[...]) - rank[2, rows_of(h), :].astype(F32)
        back[rows_of(h), :] = (up * (1.0 / TOTAL)).astype(BF)

    def stage_three(h):
        left = back[rows_of(h), :]

        def one(j, carry):
            at = pl.ds(pl.multiple_of(j * 768, 128), 768)
            up = dot_nn(left, tile_of(QI, at, 768))
            gpre[rows_of(h), at] = (up * 2.0 * relu[rows_of(h), at]).astype(BF)
            return carry

        lax.fori_loop(0, cols[QI] // 768, one, 0)

    def gram_send(h):
        sum_send(GRAM, h, w[QO][2 * h : 2 * h + 2].reshape(256, cols[QO]), QO)

    loss_acc[...] = jnp.zeros_like(loss_acc)
    loads[0].wait()
    cast(PI)
    pl.semaphore_wait(barrier, 2 * (DP - 1))
    gather_one(PI)
    loads[4].wait()
    cast(QO)
    gather_one(QO)
    loads[1].wait()
    cast(PO)
    gather_two(PI)
    gather_two(QO)
    gather_one(PO)
    loads[3].wait()
    cast(QI)
    gather_last(PI)
    gather_last(QO)
    gather_two(PO)
    gather_one(QI)
    loads[2].wait()
    loads[5].wait()
    gather_end(PI)
    stage_zero(0)
    sum_scatter(0, 0)
    stage_zero(1)
    sum_scatter(0, 1)
    gather_end(QO)
    sum_send(2, 0, tgt[rows_of(0), :], QO)
    sum_scatter(2, 0)
    sum_send(2, 1, tgt[rows_of(1), :], QO)
    sum_scatter(2, 1)
    sum_gather(0, 0)
    sum_gather(0, 1)
    gather_last(PO)
    gather_two(QI)
    gram_send(0)
    sum_scatter(GRAM, 0)
    gram_send(1)
    sum_scatter(GRAM, 1)
    sum_share(0, 0)
    sum_share(0, 1)
    gather_last(QI)
    sum_gather(2, 0)
    sum_gather(2, 1)
    gather_end(PO)
    sum_end(0, 0)
    stage_one(0)
    sum_end(0, 1)
    stage_one(1)
    sum_gather(GRAM, 0)
    sum_gather(GRAM, 1)
    sum_share(2, 0)
    sum_share(2, 1)
    gather_end(QI)
    sum_send(1, 0, hid[rows_of(0), :], QI)
    sum_scatter(1, 0)
    sum_send(1, 1, hid[rows_of(1), :], QI)
    sum_scatter(1, 1)
    sum_share(GRAM, 0)
    sum_share(GRAM, 1)
    sum_gather(1, 0)
    sum_gather(1, 1)
    sum_end(2, 0)
    sum_end(2, 1)
    sum_end(GRAM, 0)
    sum_end(GRAM, 1)
    sum_share(1, 0)
    sum_end(1, 0)
    stage_two(0)
    stage_back(0)
    sum_share(1, 1)
    sum_end(1, 1)
    stage_two(1)
    gradient(QO, rank.at[1], gout)
    scatter_one(QO)
    stage_back(1)
    gradient(QI, back, hid)
    scatter_one(QI)
    stage_three(0)
    sum_send(3, 0, gpre[rows_of(0), :], PO)
    sum_scatter(3, 0)
    stage_three(1)
    sum_send(3, 1, gpre[rows_of(1), :], PO)
    sum_scatter(3, 1)
    scatter_mid(QO)
    gradient(PO, rank.at[0], gpre)
    scatter_one(PO)
    sum_gather(3, 0)
    sum_gather(3, 1)
    scatter_mid(QI)
    sum_share(3, 0)
    sum_share(3, 1)
    scatter_two(QO)
    sum_end(3, 0)
    sum_end(3, 1)
    gradient(PI, rank.at[3], tok)
    scatter_one(PI)
    scatter_mid(PO)
    scatter_two(QI)
    squares = scatter_end(QO)
    scatter_mid(PI)
    scatter_two(PO)
    scatter_two(PI)
    squares = squares + scatter_end(QI)
    squares = squares + scatter_end(PO)
    squares = squares + scatter_end(PI)

    sc_buf[0, me_t, 0] = squares
    sc_buf[0, me_t, 1] = loss_acc[...]

    def over_tensor(k, carry):
        own = sc_buf.at[0, me_t]
        start(own, own, sc_send.at[0], sc_recv.at[0], (me_dp, lax.rem(me_t + k, TP)))
        return carry

    lax.fori_loop(1, TP, over_tensor, 0)
    wait_for(sc_buf.at[0, pl.ds(0, TP - 1)], sc_recv, (0,))
    sc_buf[1, me_dp] = jnp.sum(sc_buf[0], axis=0)

    def over_dp(k, carry):
        own = sc_buf.at[1, me_dp]
        start(own, own, sc_send.at[1], sc_recv.at[1], (lax.rem(me_dp + k, DP), me_t))
        return carry

    lax.fori_loop(1, DP, over_dp, 0)
    wait_for(sc_buf.at[1, pl.ds(0, DP - 1)], sc_recv, (1,))
    stat[...] = jnp.sum(sc_buf[1], axis=0)

    for ref, sem, spot_of in sent:
        wait_for(ref, sem, spot_of)
    for k in range(2):
        wait_for(sc_buf.at[k, pl.ds(0, TP - 1)], sc_send, (k,))


def adam_body(
    stat, g_pi, g_po, g_qi, g_qo, p_pi, p_po, p_qi, p_qo, wm, ws, hm, hs,
    n_pi, n_po, n_qi, n_qo, nwm, nws, nhm, nhs, loss,
    ga, gb, gc, gd, pa, pb, pc, pd, ma, mb, mc, md, va, vb, vc, vd, in_sem, out_sem,
):
    jobs = (
        (g_pi, p_pi, wm, ws, 0, n_pi, nwm, nws, ga, pa, ma, va),
        (g_qo, p_qo, wm, ws, 1, n_qo, nwm, nws, gd, pd, md, vd),
        (g_po, p_po, hm, hs, 0, n_po, nhm, nhs, gb, pb, mb, vb),
        (g_qi, p_qi, hm, hs, 1, n_qi, nhm, nhs, gc, pc, mc, vc),
    )
    ins, outs = [], []
    for j, (g, p, m, v, k, _, _, _, gs, ps, ms, vs) in enumerate(jobs):
        ins.append([
            pltpu.make_async_copy(src, dst, in_sem.at[j, i])
            for i, (src, dst) in enumerate(((g, gs), (p, ps), (m.at[k], ms), (v.at[k], vs)))
        ])
        for cp in ins[j]:
            cp.start()
    squares = jnp.sum(stat[0])
    scale = 1.0 / jnp.maximum(jnp.sqrt(squares), 1.0)
    loss[0, 0] = jnp.sum(stat[1]) / (2.0 * TOTAL)
    for j, (_, _, _, _, k, new_p, new_m, new_v, gs, ps, ms, vs) in enumerate(jobs):
        for cp in ins[j]:
            cp.wait()
        grad = gs[...] * scale
        mean = beta_one * ms[...] + (1.0 - beta_one) * grad
        square = beta_two * vs[...] + (1.0 - beta_two) * grad * grad
        corrected = mean * (1.0 / (1.0 - beta_one**10))
        spread = jnp.sqrt(square * (1.0 / (1.0 - beta_two**10))) + tiny_eps
        ps[...] = ps[...] - learn_rate * corrected / spread
        ms[...] = mean
        vs[...] = square
        for i, (src, dst) in enumerate(((ps, new_p), (ms, new_m.at[k]), (vs, new_v.at[k]))):
            cp = pltpu.make_async_copy(src, dst, out_sem.at[j, i])
            cp.start()
            outs.append(cp)
    for cp in outs:
        cp.wait()


def shards(
    tokens, target, first_in, first_out, second_in, second_out,
    width_mean, width_square, hidden_mean, hidden_square,
):
    wide = first_in.shape[1]
    deep = first_out.shape[1]
    cols = (wide, deep, deep, wide)
    vm = pltpu.VMEM
    dma = pltpu.SemaphoreType.DMA
    scratch = [vm((TOKD, wide), BF), vm((TOKD, wide), BF)]
    scratch += [vm((ROWS, n), F32) for n in cols]
    scratch += [vm((NX, NY, 2, 16, n), BF) for n in cols]
    scratch += [vm((NX, NY, 2, 16, n), BF) for n in cols]
    scratch += [vm((2, 3, 4, 16, n), BF) for n in cols]
    scratch += [vm((2, 4, 16, n), BF) for n in cols]
    scratch += [vm((2, 3, 16, n), BF) for n in cols]
    scratch += [vm((2, 4, 16, n), BF) for n in cols]
    scratch += [
        vm((4, TOKD, RANK), BF),
        vm((TOKD, RANK), BF),
        vm((RANK, TOKD), BF),
        vm((TOKD, deep), F32),
        vm((TOKD, deep), BF),
        vm((TOKD, deep), BF),
        vm((TOKD, wide), BF),
        vm((2, HALF, 256), F32),
        vm((4, 2, HALF, 256), BF),
        vm((4, 2, HALF, 256), BF),
        vm((4, 2, NZ, 48, 128), F32),
        vm((4, 2, NZ, 48, 128), BF),
        vm((4, 2, NZ - 1, 48, 128), BF),
        vm((RANK, RANK), BF),
        vm((2, 256, 256), F32),
        vm((2, 256, 256), BF),
        vm((2, 256, 256), BF),
        vm((2, NZ, 64, 128), F32),
        vm((2, NZ, 64, 128), BF),
        vm((2, NZ - 1, 64, 128), BF),
        vm((8, 128), F32),
        vm((2, 16, 2, 8, 128), F32),
        dma((6,)),
        dma((4, 3, 2, 3)), dma((4, 3, 2, 3)),
        dma((4, 4, 2, 3)), dma((4, 4, 2, 3)),
        dma((5, 2, 4)), dma((5, 2, 4)),
        dma((2,)), dma((2,)),
    ]
    whole = pl.BlockSpec(memory_space=pltpu.VMEM)
    g_pi, g_po, g_qi, g_qo, stat = pl.pallas_call(
        body,
        name="step",
        out_shape=[jax.ShapeDtypeStruct((ROWS, n), F32) for n in cols]
        + [jax.ShapeDtypeStruct((2, 8, 128), F32)],
        in_specs=[pl.BlockSpec(memory_space=pl.ANY)] * 6,
        out_specs=[whole] * 5,
        scratch_shapes=scratch,
        compiler_params=pltpu.CompilerParams(
            collective_id=0, has_side_effects=True, vmem_limit_bytes=58 * 2**20
        ),
    )(tokens, target, first_in, first_out, second_in, second_out)

    anywhere = pl.BlockSpec(memory_space=pl.ANY)
    outs = pl.pallas_call(
        adam_body,
        name="adam",
        out_shape=[jax.ShapeDtypeStruct((ROWS, n), F32) for n in cols]
        + [jax.ShapeDtypeStruct((2, ROWS, n), F32) for n in (wide, wide, deep, deep)]
        + [jax.ShapeDtypeStruct((1, 1), F32)],
        in_specs=[whole] + [anywhere] * 12,
        out_specs=[anywhere] * 8 + [pl.BlockSpec(memory_space=pltpu.SMEM)],
        scratch_shapes=[vm((ROWS, n), F32) for n in cols] * 4 + [dma((4, 4)), dma((4, 3))],
        compiler_params=pltpu.CompilerParams(vmem_limit_bytes=60 * 2**20),
    )(
        stat, g_pi, g_po, g_qi, g_qo, first_in, first_out, second_in, second_out,
        width_mean, width_square, hidden_mean, hidden_square,
    )
    return tuple(outs[:8]) + (outs[8].reshape(()),)


def solution(mesh):
    two = P("dp", "tensor")
    three = P(None, "dp", "tensor")
    return jax.shard_map(
        shards,
        mesh=mesh,
        in_specs=(two,) * 6 + (three,) * 4,
        out_specs=(two,) * 4 + (three,) * 4 + (P(),),
        check_vma=False,
    )
```

```python
import functools

import jax
import jax.numpy as jnp
from jax import lax
from jax.experimental import pallas as pl
from jax.experimental.pallas import tpu as pltpu
from jax.sharding import PartitionSpec as P

beta_one = 0.9
beta_two = 0.95
learn_rate = 0.1
tiny_eps = 1e-08

MESH = pl.DeviceIdType.MESH
BF = jnp.bfloat16
F32 = jnp.float32

NX, NY, NZ = 4, 4, 8
DP = NX * NY
TP = NZ * 2
ROWS = 32
RANK = DP * ROWS
TOKD = 384
HALF = TOKD // 2
TOTAL = TOKD * DP
PI, PO, QI, QO = 0, 1, 2, 3
GRAM = 4


def dot_nt(left, right):
    return lax.dot_general(
        left, right, (((1,), (1,)), ((), ())), preferred_element_type=F32
    )


def dot_nn(left, right):
    return jnp.dot(left, right, preferred_element_type=F32)


def body(
    tokens, target, fi, fo, si, so,
    g_pi, g_po, g_qi, g_qo, stat,
    tok, tgt, wf0, wf1, wf2, wf3,
    w0, w1, w2, w3, gr0, gr1, gr2, gr3,
    ra0, ra1, ra2, ra3, rb0, rb1, rb2, rb3, rc0, rc1, rc2, rc3,
    cb0, cb1, cb2, cb3, cc0, cc1, cc2, cc3,
    rank, back, ranks_t, relu, hid, gpre, gout, partial,
    sib_send, sib_recv, z_keep, z_send, z_recv,
    gram, gpartial, gsib_send, gsib_recv, gz_keep, gz_send, gz_recv, loss_acc, sc_buf,
    ld_sem, ag_send, ag_recv, rs_send, rs_recv, ar_send, ar_recv, gr_send, gr_recv, sc_send, sc_recv,
):
    me_dp = lax.axis_index("dp")
    me_t = lax.axis_index("tensor")
    x, y = me_dp // NY, lax.rem(me_dp, NY)
    z, c = me_t // 2, lax.rem(me_t, 2)
    wf = (wf0, wf1, wf2, wf3)
    w = (w0, w1, w2, w3)
    gr = (gr0, gr1, gr2, gr3)
    ra = (ra0, ra1, ra2, ra3)
    rb = (rb0, rb1, rb2, rb3)
    rc = (rc0, rc1, rc2, rc3)
    cb = (cb0, cb1, cb2, cb3)
    cc = (cc0, cc1, cc2, cc3)
    gouts = (g_pi, g_po, g_qi, g_qo)
    cols = tuple(r.shape[-1] for r in wf)

    def at_x(d):
        return (lax.rem(x + d, NX) * NY + y, me_t)

    def at_y(d):
        return (x * NY + lax.rem(y + d, NY), me_t)

    def at_z(d):
        return (me_dp, lax.rem(z + d, NZ) * 2 + c)

    sibling = (me_dp, z * 2 + 1 - c)

    sent = []

    def start(src, dst, s_sem, r_sem, where):
        pltpu.make_async_remote_copy(
            src_ref=src, dst_ref=dst, send_sem=s_sem, recv_sem=r_sem,
            device_id=where, device_id_type=MESH,
        ).start()

    def send(src, dst, sems, spot_of, where):
        start(src, dst, sems[0].at[spot_of], sems[1].at[spot_of], where)
        sent.append((src, sems[0], spot_of))

    def wait_for(ref, sem, spot_of):
        at = sem.at[spot_of]
        pltpu.make_async_copy(ref, ref, at).wait()

    ag = (ag_send, ag_recv)
    rs = (rs_send, rs_recv)
    ar = (ar_send, ar_recv)
    low, high = pl.ds(0, 2), pl.ds(2, 2)

    def cut(a):
        n = cols[a] // 256 * 128
        return pl.ds(0, n), pl.ds(n, cols[a] - n)

    def around(m):
        return lax.rem(m + 1, 4), lax.rem(m + 2, 4), lax.rem(m + 3, 4)

    barrier = pltpu.get_barrier_semaphore()

    def greet(k, carry):
        pl.semaphore_signal(
            barrier, inc=1, device_id=(lax.rem(me_dp + k, DP), me_t), device_id_type=MESH
        )
        pl.semaphore_signal(
            barrier, inc=1, device_id=(me_dp, lax.rem(me_t + k, TP)), device_id_type=MESH
        )
        return carry

    lax.fori_loop(1, DP, greet, 0, unroll=True)

    loads = [
        pltpu.make_async_copy(s, d, ld_sem.at[k])
        for k, (s, d) in enumerate(
            ((fi, wf0), (fo, wf1), (tokens, tok), (si, wf2), (so, wf3), (target, tgt))
        )
    ]
    for cp in loads:
        cp.start()

    def cast(a):
        w[a][x, y] = wf[a][...].astype(BF).reshape(2, 16, cols[a])

    def slot(a, half, p, q, part=slice(None)):
        if half == 0:
            return w[a].at[p, q, 0, :, part]
        return w[a].at[q, p, 1, :, part]

    def places(half):
        return (x, y, at_x, at_y) if half == 0 else (y, x, at_y, at_x)

    def gather_one(a):
        for half in range(2):
            m, q, go, _ = places(half)
            own = slot(a, half, m, q)
            for d in (2, 1, 3):
                send(own, own, ag, (a, 0, half, d - 1), go(d))

    def gather_two(a):
        for half in range(2):
            m, q, _, go = places(half)
            for d in range(3):
                wait_for(slot(a, half, m, q), ag_recv, (a, 0, half, d))
            row = slot(a, half, pl.ds(0, 4), q)
            send(row, row, ag, (a, 1, half, 0), go(1))
            send(row, row, ag, (a, 1, half, 1), go(3))

    def gather_all(a):
        for half in range(2):
            m, q, _, go = places(half)
            for d in range(3):
                wait_for(slot(a, half, m, q), ag_recv, (a, 0, half, d))
            row = slot(a, half, pl.ds(0, 4), q)
            for d in (2, 1, 3):
                send(row, row, ag, (a, 1, half, d - 1), go(d))

    def gather_done(a):
        for half in range(2):
            _, q, _, _ = places(half)
            for d in range(3):
                wait_for(slot(a, half, pl.ds(0, 4), q), ag_recv, (a, 1, half, d))

    def gather_last(a):
        for half in range(2):
            _, q, _, go = places(half)
            right, _, left = around(q)
            wait_for(slot(a, half, pl.ds(0, 4), left), ag_recv, (a, 1, half, 0))
            part = slot(a, half, low, left)
            send(part, part, ag, (a, 2, half, 0), go(1))
            wait_for(slot(a, half, pl.ds(0, 4), right), ag_recv, (a, 1, half, 1))
            part = slot(a, half, high, right)
            send(part, part, ag, (a, 2, half, 1), go(3))

    def gather_end(a):
        for half in range(2):
            _, q, _, _ = places(half)
            _, far, _ = around(q)
            wait_for(slot(a, half, low, far), ag_recv, (a, 2, half, 0))
            wait_for(slot(a, half, high, far), ag_recv, (a, 2, half, 1))

    gram_rows = pl.ds(pl.multiple_of(x * 128, 128), 128)

    def set_of(s):
        if s == GRAM:
            return gsib_send, gsib_recv, gz_keep, gz_send, gz_recv, gram.at[gram_rows], gpartial
        return (
            sib_send.at[s], sib_recv.at[s], z_keep.at[s], z_send.at[s], z_recv.at[s], rank.at[s], partial,
        )

    def sum_send(s, h, left, a):
        out, into, _, _, _, _, keep = set_of(s)
        n = 1 - c
        out[h] = dot_nt(left, w[a][pl.ds(2 * n, 2)].reshape(256, cols[a])).astype(BF)
        send(out.at[h], into.at[h], ar, (s, h, 0), sibling)
        keep[h] = dot_nt(left, w[a][pl.ds(2 * c, 2)].reshape(256, cols[a]))

    def sum_scatter(s, h):
        _, into, own, out, there, _, keep = set_of(s)
        tall = out.shape[2]
        wait_for(into.at[h], ar_recv, (s, h, 0))
        both = keep[h] + into[h].astype(F32)
        for k in range(NZ):
            zr, zc = k // 2, k % 2
            piece = both[zr * tall : (zr + 1) * tall, zc * 128 : (zc + 1) * 128]
            own[h, k] = piece
            out[h, k] = piece.astype(BF)

        def one(i, carry):
            d = lax.rem(i + 3, NZ - 1) + 1
            start(
                out.at[h, lax.rem(z + d, NZ)], there.at[h, d - 1],
                ar_send.at[s, h, 1], ar_recv.at[s, h, 1], at_z(d),
            )
            return carry

        lax.fori_loop(0, NZ - 1, one, 0, unroll=True)
        sent.append((there.at[h], ar_send, (s, h, 1)))

    def sum_gather(s, h):
        _, _, own, _, there, result, _ = set_of(s)
        tall = own.shape[2]
        wait_for(there.at[h], ar_recv, (s, h, 1))
        total = own[h, z]
        for k in range(NZ - 1):
            total = total + there[h, k].astype(F32)
        row = pl.multiple_of(h * 4 * tall + (z // 2) * tall, 16)
        col = pl.multiple_of(c * 256 + lax.rem(z, 2) * 128, 128)
        mine = result.at[pl.ds(row, tall), pl.ds(col, 128)]
        mine[...] = total.astype(BF)

        def one(i, carry):
            d = lax.rem(i + 3, NZ - 1) + 1
            start(mine, mine, ar_send.at[s, h, 2], ar_recv.at[s, h, 2], at_z(d))
            return carry

        lax.fori_loop(0, NZ - 1, one, 0, unroll=True)
        sent.append((there.at[h], ar_send, (s, h, 2)))

    def half_of(s, h):
        _, _, own, _, _, result, _ = set_of(s)
        tall = own.shape[2]
        col = pl.multiple_of(c * 256, 128)
        return result.at[pl.ds(h * 4 * tall, 4 * tall), pl.ds(col, 256)]

    def sum_share(s, h):
        there = set_of(s)[4]
        wait_for(there.at[h], ar_recv, (s, h, 2))
        part = half_of(s, h)
        send(part, part, ar, (s, h, 3), sibling)

    def sum_end(s, h):
        wait_for(half_of(s, h), ar_recv, (s, h, 3))

    def piece(a, half, t, part):
        return gr[a].at[part, t, 0] if half == 0 else gr[a].at[t, part, 1]

    def add_blocks(out, first, terms, count):
        def one(k, carry):
            total = first(k)[...].astype(F32)
            for term in terms:
                total = total + term(k)[...].astype(F32)
            out(k)[...] = total.astype(BF)
            return carry

        lax.fori_loop(0, count, one, 0)

    def scatter_one(a):
        for half in range(2):
            _, m, _, go = places(half)
            right, far, left = around(m)
            send(piece(a, half, far, low), ra[a].at[half, 0, low], rs, (a, 0, half, 0), go(1))
            send(piece(a, half, far, high), ra[a].at[half, 0, high], rs, (a, 0, half, 1), go(3))
            send(piece(a, half, right, high), ra[a].at[half, 1, high], rs, (a, 1, half, 0), go(1))
            send(piece(a, half, left, low), ra[a].at[half, 1, low], rs, (a, 1, half, 1), go(3))

    def scatter_mid(a):
        for half in range(2):
            _, m, _, go = places(half)
            right, _, left = around(m)
            for side, (part, base, to, d) in enumerate(((low, 0, right, 1), (high, 2, left, 3))):
                wait_for(ra[a].at[half, 0, part], rs_recv, (a, 0, half, side))
                add_blocks(
                    lambda k: cb[a].at[half, base + k],
                    lambda k: piece(a, half, to, base + k),
                    (lambda k: ra[a].at[half, 0, base + k],),
                    2,
                )
                send(cb[a].at[half, part], ra[a].at[half, 2, part], rs, (a, 2, half, side), go(d))

    def scatter_two(a):
        for half in range(2):
            q, m, go, _ = places(half)
            wait_for(ra[a].at[half, 1, high], rs_recv, (a, 1, half, 0))
            wait_for(ra[a].at[half, 1, low], rs_recv, (a, 1, half, 1))
            wait_for(ra[a].at[half, 2, low], rs_recv, (a, 2, half, 0))
            wait_for(ra[a].at[half, 2, high], rs_recv, (a, 2, half, 1))
            add_blocks(
                lambda k: rb[a].at[half, k],
                lambda k: piece(a, half, m, k),
                (lambda k: ra[a].at[half, 1, k], lambda k: ra[a].at[half, 2, k]),
                4,
            )
            for d in (2, 1, 3):
                send(
                    rb[a].at[half, lax.rem(q + d, 4)], rc[a].at[half, d - 1],
                    rs, (a, 3, half, d - 1), go(d),
                )

    def scatter_near(a):
        left_cols, right_cols = cut(a)
        for half in range(2):
            q, m, go, _ = places(half)
            wait_for(ra[a].at[half, 1, high], rs_recv, (a, 1, half, 0))
            wait_for(ra[a].at[half, 1, low], rs_recv, (a, 1, half, 1))
            wait_for(ra[a].at[half, 2, low], rs_recv, (a, 2, half, 0))
            wait_for(ra[a].at[half, 2, high], rs_recv, (a, 2, half, 1))
            add_blocks(
                lambda k: rb[a].at[half, k],
                lambda k: piece(a, half, m, k),
                (lambda k: ra[a].at[half, 1, k], lambda k: ra[a].at[half, 2, k]),
                4,
            )
            right, far, left = around(q)
            for kind, side, owner, part, d in (
                (0, 0, far, left_cols, 1),
                (0, 1, far, right_cols, 3),
                (1, 0, right, right_cols, 1),
                (1, 1, left, left_cols, 3),
            ):
                send(
                    rb[a].at[half, owner, :, part], rc[a].at[half, kind, :, part],
                    rs, (a, 3 + kind, half, side), go(d),
                )

    def scatter_late(a):
        left_cols, right_cols = cut(a)
        for half in range(2):
            q, _, go, _ = places(half)
            right, _, left = around(q)
            for side, (part, owner, d) in enumerate(((left_cols, right, 1), (right_cols, left, 3))):
                wait_for(rc[a].at[half, 0, :, part], rs_recv, (a, 3, half, side))
                total = rb[a][half, owner, :, part].astype(F32) + rc[a][half, 0, :, part].astype(F32)
                cc[a][half, :, part] = total.astype(BF)
                send(
                    cc[a].at[half, :, part], rc[a].at[half, 2, :, part],
                    rs, (a, 5, half, side), go(d),
                )

    def scatter_done(a):
        left_cols, right_cols = cut(a)
        squares = jnp.zeros((8, 128), F32)
        for half in range(2):
            q, _, _, _ = places(half)
            wait_for(rc[a].at[half, 1, :, right_cols], rs_recv, (a, 4, half, 0))
            wait_for(rc[a].at[half, 1, :, left_cols], rs_recv, (a, 4, half, 1))
            wait_for(rc[a].at[half, 2, :, left_cols], rs_recv, (a, 5, half, 0))
            wait_for(rc[a].at[half, 2, :, right_cols], rs_recv, (a, 5, half, 1))
            total = rb[a][half, q].astype(F32) + rc[a][half, 1].astype(F32) + rc[a][half, 2].astype(F32)
            gouts[a][half * 16 : (half + 1) * 16, :] = total
            sq = total * total
            sq = sq[0:8] + sq[8:16]
            for j in range(cols[a] // 128):
                squares = squares + sq[:, j * 128 : (j + 1) * 128]
        return squares

    def scatter_end(a):
        squares = jnp.zeros((8, 128), F32)
        for half in range(2):
            q, _, _, _ = places(half)
            total = rb[a][half, q].astype(F32)
            for d in range(3):
                wait_for(rc[a].at[half, d], rs_recv, (a, 3, half, d))
                total = total + rc[a][half, d].astype(F32)
            gouts[a][half * 16 : (half + 1) * 16, :] = total
            sq = total * total
            sq = sq[0:8] + sq[8:16]
            for j in range(cols[a] // 128):
                squares = squares + sq[:, j * 128 : (j + 1) * 128]
        return squares

    def gradient(a, left, right):
        ranks_t[...] = left[...].T
        step = 768 if cols[a] % 768 == 0 else 384

        def one(j, carry):
            at = pl.ds(pl.multiple_of(j * step, 128), step)
            tile = dot_nn(ranks_t[...], right[:, at]).astype(BF)
            gr[a][:, :, :, :, at] = tile.reshape(NX, NY, 2, 16, step)
            return carry

        lax.fori_loop(0, cols[a] // step, one, 0)

    def tile_of(a, at, n):
        return w[a][:, :, :, :, at].reshape(RANK, n)

    def rows_of(h):
        return pl.ds(h * HALF, HALF)

    def stage_zero(h):
        sum_send(0, h, tok[rows_of(h), :], PI)

    def stage_one(h):
        left = rank[0, rows_of(h), :]

        def one(j, carry):
            at = pl.ds(pl.multiple_of(j * 768, 128), 768)
            pre = jnp.maximum(dot_nn(left, tile_of(PO, at, 768)), 0.0)
            relu[rows_of(h), at] = pre
            hid[rows_of(h), at] = (pre * pre).astype(BF)
            return carry

        lax.fori_loop(0, cols[PO] // 768, one, 0)

    def stage_two(h):
        left = rank[1, rows_of(h), :]

        def one(j, carry):
            at = pl.ds(pl.multiple_of(j * 384, 128), 384)
            misfit = dot_nn(left, tile_of(QO, at, 384)) - tgt[rows_of(h), at].astype(F32)
            gout[rows_of(h), at] = (misfit * (1.0 / TOTAL)).astype(BF)
            sq = (misfit * misfit).reshape(HALF // 8, 8, 384).sum(axis=0)
            loss_acc[...] += sq[:, 0:128] + sq[:, 128:256] + sq[:, 256:384]
            return carry

        lax.fori_loop(0, cols[QO] // 384, one, 0)

    def stage_back(h):
        up = dot_nn(rank[1, rows_of(h), :], gram[...]) - rank[2, rows_of(h), :].astype(F32)
        back[rows_of(h), :] = (up * (1.0 / TOTAL)).astype(BF)

    def stage_three(h):
        left = back[rows_of(h), :]

        def one(j, carry):
            at = pl.ds(pl.multiple_of(j * 768, 128), 768)
            up = dot_nn(left, tile_of(QI, at, 768))
            gpre[rows_of(h), at] = (up * 2.0 * relu[rows_of(h), at]).astype(BF)
            return carry

        lax.fori_loop(0, cols[QI] // 768, one, 0)

    def gram_send():
        sum_send(GRAM, 0, w[QO][x].reshape(128, cols[QO]), QO)

    def gram_spread():
        part = gram.at[gram_rows]
        for d in (2, 1, 3):
            send(part, part, (gr_send, gr_recv), (d - 1,), at_x(d))

    def gram_end():
        for d in range(3):
            wait_for(gram.at[gram_rows], gr_recv, (d,))

    loss_acc[...] = jnp.zeros_like(loss_acc)
    loads[0].wait()
    cast(PI)
    pl.semaphore_wait(barrier, 2 * (DP - 1))
    gather_one(PI)
    loads[4].wait()
    cast(QO)
    gather_one(QO)
    loads[1].wait()
    cast(PO)
    gather_two(PI)
    gather_two(QO)
    gather_one(PO)
    loads[3].wait()
    cast(QI)
    gather_last(PI)
    gather_last(QO)
    gather_two(PO)
    gather_one(QI)
    loads[2].wait()
    loads[5].wait()
    gather_end(PI)
    stage_zero(0)
    sum_scatter(0, 0)
    stage_zero(1)
    sum_scatter(0, 1)
    sum_gather(0, 0)
    sum_gather(0, 1)
    gather_last(PO)
    gather_all(QI)
    gather_end(QO)
    gram_send()
    sum_scatter(GRAM, 0)
    sum_send(2, 0, tgt[rows_of(0), :], QO)
    sum_scatter(2, 0)
    sum_send(2, 1, tgt[rows_of(1), :], QO)
    sum_scatter(2, 1)
    sum_share(0, 0)
    sum_share(0, 1)
    sum_gather(2, 0)
    sum_gather(2, 1)
    sum_gather(GRAM, 0)
    gather_end(PO)
    sum_end(0, 0)
    stage_one(0)
    sum_end(0, 1)
    stage_one(1)
    sum_share(2, 0)
    sum_share(2, 1)
    sum_share(GRAM, 0)
    gather_done(QI)
    sum_send(1, 0, hid[rows_of(0), :], QI)
    sum_scatter(1, 0)
    sum_send(1, 1, hid[rows_of(1), :], QI)
    sum_scatter(1, 1)
    sum_end(GRAM, 0)
    gram_spread()
    sum_gather(1, 0)
    sum_gather(1, 1)
    sum_end(2, 0)
    sum_end(2, 1)
    gram_end()
    sum_share(1, 0)
    sum_end(1, 0)
    stage_two(0)
    stage_back(0)
    sum_share(1, 1)
    sum_end(1, 1)
    stage_two(1)
    gradient(QO, rank.at[1], gout)
    scatter_one(QO)
    stage_back(1)
    gradient(QI, back, hid)
    scatter_one(QI)
    stage_three(0)
    sum_send(3, 0, gpre[rows_of(0), :], PO)
    sum_scatter(3, 0)
    stage_three(1)
    sum_send(3, 1, gpre[rows_of(1), :], PO)
    sum_scatter(3, 1)
    scatter_mid(QO)
    gradient(PO, rank.at[0], gpre)
    scatter_one(PO)
    sum_gather(3, 0)
    sum_gather(3, 1)
    scatter_mid(QI)
    sum_share(3, 0)
    sum_share(3, 1)
    scatter_near(QO)
    sum_end(3, 0)
    sum_end(3, 1)
    gradient(PI, rank.at[3], tok)
    scatter_one(PI)
    scatter_late(QO)
    scatter_mid(PO)
    scatter_near(QI)
    scatter_mid(PI)
    scatter_near(PO)
    scatter_late(QI)
    squares = scatter_done(QO)
    scatter_two(PI)
    scatter_late(PO)
    squares = squares + scatter_done(QI)
    squares = squares + scatter_done(PO)
    squares = squares + scatter_end(PI)

    sc_buf[0, me_t, 0] = squares
    sc_buf[0, me_t, 1] = loss_acc[...]

    def over_tensor(k, carry):
        own = sc_buf.at[0, me_t]
        start(own, own, sc_send.at[0], sc_recv.at[0], (me_dp, lax.rem(me_t + k, TP)))
        return carry

    lax.fori_loop(1, TP, over_tensor, 0, unroll=True)
    wait_for(sc_buf.at[0, pl.ds(0, TP - 1)], sc_recv, (0,))
    sc_buf[1, me_dp] = jnp.sum(sc_buf[0], axis=0)

    def over_dp(k, carry):
        own = sc_buf.at[1, me_dp]
        start(own, own, sc_send.at[1], sc_recv.at[1], (lax.rem(me_dp + k, DP), me_t))
        return carry

    lax.fori_loop(1, DP, over_dp, 0, unroll=True)
    wait_for(sc_buf.at[1, pl.ds(0, DP - 1)], sc_recv, (1,))
    stat[...] = jnp.sum(sc_buf[1], axis=0)

    for ref, sem, spot_of in sent:
        wait_for(ref, sem, spot_of)
    for k in range(2):
        wait_for(sc_buf.at[k, pl.ds(0, TP - 1)], sc_send, (k,))


def adam_body(
    stat, g_pi, g_po, g_qi, g_qo, p_pi, p_po, p_qi, p_qo, wm, ws, hm, hs,
    n_pi, n_po, n_qi, n_qo, nwm, nws, nhm, nhs, loss,
):
    squares = jnp.sum(stat[0])
    scale = 1.0 / jnp.maximum(jnp.sqrt(squares), 1.0)
    loss[0, 0] = jnp.sum(stat[1]) / (2.0 * TOTAL)
    for g, p, m, v, k, new_p, new_m, new_v in (
        (g_pi, p_pi, wm, ws, 0, n_pi, nwm, nws),
        (g_qo, p_qo, wm, ws, 1, n_qo, nwm, nws),
        (g_po, p_po, hm, hs, 0, n_po, nhm, nhs),
        (g_qi, p_qi, hm, hs, 1, n_qi, nhm, nhs),
    ):
        grad = g[...] * scale
        mean = beta_one * m[k] + (1.0 - beta_one) * grad
        square = beta_two * v[k] + (1.0 - beta_two) * grad * grad
        corrected = mean * (1.0 / (1.0 - beta_one**10))
        spread = jnp.sqrt(square * (1.0 / (1.0 - beta_two**10))) + tiny_eps
        new_p[...] = p[...] - learn_rate * corrected / spread
        new_m[k] = mean
        new_v[k] = square


def shards(
    tokens, target, first_in, first_out, second_in, second_out,
    width_mean, width_square, hidden_mean, hidden_square,
):
    wide = first_in.shape[1]
    deep = first_out.shape[1]
    cols = (wide, deep, deep, wide)
    vm = pltpu.VMEM
    dma = pltpu.SemaphoreType.DMA
    scratch = [vm((TOKD, wide), BF), vm((TOKD, wide), BF)]
    scratch += [vm((ROWS, n), F32) for n in cols]
    scratch += [vm((NX, NY, 2, 16, n), BF) for n in cols]
    scratch += [vm((NX, NY, 2, 16, n), BF) for n in cols]
    scratch += [vm((2, 3, 4, 16, n), BF) for n in cols]
    scratch += [vm((2, 4, 16, n), BF) for n in cols]
    scratch += [vm((2, 3, 16, n), BF) for n in cols]
    scratch += [vm((2, 4, 16, n), BF) for n in cols]
    scratch += [vm((2, 16, n), BF) for n in cols]
    scratch += [
        vm((4, TOKD, RANK), BF),
        vm((TOKD, RANK), BF),
        vm((RANK, TOKD), BF),
        vm((TOKD, deep), F32),
        vm((TOKD, deep), BF),
        vm((TOKD, deep), BF),
        vm((TOKD, wide), BF),
        vm((2, HALF, 256), F32),
        vm((4, 2, HALF, 256), BF),
        vm((4, 2, HALF, 256), BF),
        vm((4, 2, NZ, 48, 128), F32),
        vm((4, 2, NZ, 48, 128), BF),
        vm((4, 2, NZ - 1, 48, 128), BF),
        vm((RANK, RANK), BF),
        vm((1, 128, 256), F32),
        vm((1, 128, 256), BF),
        vm((1, 128, 256), BF),
        vm((1, NZ, 32, 128), F32),
        vm((1, NZ, 32, 128), BF),
        vm((1, NZ - 1, 32, 128), BF),
        vm((8, 128), F32),
        vm((2, 16, 2, 8, 128), F32),
        dma((6,)),
        dma((4, 3, 2, 3)), dma((4, 3, 2, 3)),
        dma((4, 6, 2, 3)), dma((4, 6, 2, 3)),
        dma((5, 2, 4)), dma((5, 2, 4)),
        dma((3,)), dma((3,)),
        dma((2,)), dma((2,)),
    ]
    whole = pl.BlockSpec(memory_space=pltpu.VMEM)
    g_pi, g_po, g_qi, g_qo, stat = pl.pallas_call(
        body,
        name="step",
        out_shape=[jax.ShapeDtypeStruct((ROWS, n), F32) for n in cols]
        + [jax.ShapeDtypeStruct((2, 8, 128), F32)],
        in_specs=[pl.BlockSpec(memory_space=pl.ANY)] * 6,
        out_specs=[whole] * 5,
        scratch_shapes=scratch,
        compiler_params=pltpu.CompilerParams(
            collective_id=0, has_side_effects=True, vmem_limit_bytes=58 * 2**20
        ),
    )(tokens, target, first_in, first_out, second_in, second_out)

    outs = pl.pallas_call(
        adam_body,
        name="adam",
        out_shape=[jax.ShapeDtypeStruct((ROWS, n), F32) for n in cols]
        + [jax.ShapeDtypeStruct((2, ROWS, n), F32) for n in (wide, wide, deep, deep)]
        + [jax.ShapeDtypeStruct((1, 1), F32)],
        in_specs=[whole] * 13,
        out_specs=[whole] * 8 + [pl.BlockSpec(memory_space=pltpu.SMEM)],
        compiler_params=pltpu.CompilerParams(vmem_limit_bytes=60 * 2**20),
    )(
        stat, g_pi, g_po, g_qi, g_qo, first_in, first_out, second_in, second_out,
        width_mean, width_square, hidden_mean, hidden_square,
    )
    return tuple(outs[:8]) + (outs[8].reshape(()),)


def solution(mesh):
    two = P("dp", "tensor")
    three = P(None, "dp", "tensor")
    return jax.shard_map(
        shards,
        mesh=mesh,
        in_specs=(two,) * 6 + (three,) * 4,
        out_specs=(two,) * 4 + (three,) * 4 + (P(),),
        check_vma=False,
    )
```

```python
import functools

import jax
import jax.numpy as jnp
from jax import lax
from jax.experimental import pallas as pl
from jax.experimental.pallas import tpu as pltpu
from jax.sharding import PartitionSpec as P

beta_one = 0.9
beta_two = 0.95
learn_rate = 0.1
tiny_eps = 1e-08

MESH = pl.DeviceIdType.MESH
BF = jnp.bfloat16
F32 = jnp.float32

NX, NY, NZ = 4, 4, 8
DP = NX * NY
TP = NZ * 2
ROWS = 32
RANK = DP * ROWS
TOKD = 384
HALF = TOKD // 2
TOTAL = TOKD * DP
PI, PO, QI, QO = 0, 1, 2, 3
GRAM = 4


def dot_nt(left, right):
    return lax.dot_general(
        left, right, (((1,), (1,)), ((), ())), preferred_element_type=F32
    )


def dot_nn(left, right):
    return jnp.dot(left, right, preferred_element_type=F32)


def body(
    tokens, target, fi, fo, si, so,
    g_pi, g_po, g_qi, g_qo, stat,
    tok, tgt, wf0, wf1, wf2, wf3,
    w0, w1, w2, w3, gr0, gr1, gr2, gr3,
    ra0, ra1, ra2, ra3, rb0, rb1, rb2, rb3, rc0, rc1, rc2, rc3,
    cb0, cb1, cb2, cb3, cc0, cc1, cc2, cc3,
    rank, back, ranks_t, relu, hid, gpre, gout, partial,
    sib_send, sib_recv, z_keep, z_send, z_recv,
    gram, gpartial, gsib_send, gsib_recv, gz_keep, gz_send, gz_recv, loss_acc, sc_buf,
    ld_sem, ag_send, ag_recv, rs_send, rs_recv, ar_send, ar_recv, gr_send, gr_recv, sc_send, sc_recv,
):
    me_dp = lax.axis_index("dp")
    me_t = lax.axis_index("tensor")
    x, y = me_dp // NY, lax.rem(me_dp, NY)
    z, c = me_t // 2, lax.rem(me_t, 2)
    wf = (wf0, wf1, wf2, wf3)
    w = (w0, w1, w2, w3)
    gr = (gr0, gr1, gr2, gr3)
    ra = (ra0, ra1, ra2, ra3)
    rb = (rb0, rb1, rb2, rb3)
    rc = (rc0, rc1, rc2, rc3)
    cb = (cb0, cb1, cb2, cb3)
    cc = (cc0, cc1, cc2, cc3)
    gouts = (g_pi, g_po, g_qi, g_qo)
    cols = tuple(r.shape[-1] for r in wf)

    def at_x(d):
        return (lax.rem(x + d, NX) * NY + y, me_t)

    def at_y(d):
        return (x * NY + lax.rem(y + d, NY), me_t)

    def at_z(d):
        return (me_dp, lax.rem(z + d, NZ) * 2 + c)

    sibling = (me_dp, z * 2 + 1 - c)

    sent = []

    def start(src, dst, s_sem, r_sem, where):
        pltpu.make_async_remote_copy(
            src_ref=src, dst_ref=dst, send_sem=s_sem, recv_sem=r_sem,
            device_id=where, device_id_type=MESH,
        ).start()

    def send(src, dst, sems, spot_of, where):
        start(src, dst, sems[0].at[spot_of], sems[1].at[spot_of], where)
        sent.append((src, sems[0], spot_of))

    def wait_for(ref, sem, spot_of):
        at = sem.at[spot_of]
        pltpu.make_async_copy(ref, ref, at).wait()

    ag = (ag_send, ag_recv)
    rs = (rs_send, rs_recv)
    ar = (ar_send, ar_recv)
    low, high = pl.ds(0, 2), pl.ds(2, 2)

    def cut(a):
        n = cols[a] // 256 * 128
        return pl.ds(0, n), pl.ds(n, cols[a] - n)

    def around(m):
        return lax.rem(m + 1, 4), lax.rem(m + 2, 4), lax.rem(m + 3, 4)

    barrier = pltpu.get_barrier_semaphore()

    def greet(k, carry):
        pl.semaphore_signal(
            barrier, inc=1, device_id=(lax.rem(me_dp + k, DP), me_t), device_id_type=MESH
        )
        pl.semaphore_signal(
            barrier, inc=1, device_id=(me_dp, lax.rem(me_t + k, TP)), device_id_type=MESH
        )
        return carry

    lax.fori_loop(1, DP, greet, 0, unroll=True)

    loads = [
        pltpu.make_async_copy(s, d, ld_sem.at[k])
        for k, (s, d) in enumerate(
            ((fi, wf0), (fo, wf1), (tokens, tok), (si, wf2), (so, wf3), (target, tgt))
        )
    ]
    for cp in loads:
        cp.start()

    def cast(a):
        w[a][x, y] = wf[a][...].astype(BF).reshape(2, 16, cols[a])

    def slot(a, half, p, q, part=slice(None)):
        if half == 0:
            return w[a].at[p, q, 0, :, part]
        return w[a].at[q, p, 1, :, part]

    def places(half):
        return (x, y, at_x, at_y) if half == 0 else (y, x, at_y, at_x)

    def gather_one(a):
        for half in range(2):
            m, q, go, _ = places(half)
            own = slot(a, half, m, q)
            for d in (2, 1, 3):
                send(own, own, ag, (a, 0, half, d - 1), go(d))

    def gather_two(a):
        for half in range(2):
            m, q, _, go = places(half)
            for d in range(3):
                wait_for(slot(a, half, m, q), ag_recv, (a, 0, half, d))
            row = slot(a, half, pl.ds(0, 4), q)
            send(row, row, ag, (a, 1, half, 0), go(1))
            send(row, row, ag, (a, 1, half, 1), go(3))

    def gather_all(a):
        for half in range(2):
            m, q, _, go = places(half)
            for d in range(3):
                wait_for(slot(a, half, m, q), ag_recv, (a, 0, half, d))
            row = slot(a, half, pl.ds(0, 4), q)
            for d in (2, 1, 3):
                send(row, row, ag, (a, 1, half, d - 1), go(d))

    def gather_done(a):
        for half in range(2):
            _, q, _, _ = places(half)
            for d in range(3):
                wait_for(slot(a, half, pl.ds(0, 4), q), ag_recv, (a, 1, half, d))

    def gather_last(a):
        for half in range(2):
            _, q, _, go = places(half)
            right, _, left = around(q)
            wait_for(slot(a, half, pl.ds(0, 4), left), ag_recv, (a, 1, half, 0))
            part = slot(a, half, low, left)
            send(part, part, ag, (a, 2, half, 0), go(1))
            wait_for(slot(a, half, pl.ds(0, 4), right), ag_recv, (a, 1, half, 1))
            part = slot(a, half, high, right)
            send(part, part, ag, (a, 2, half, 1), go(3))

    def gather_end(a):
        for half in range(2):
            _, q, _, _ = places(half)
            _, far, _ = around(q)
            wait_for(slot(a, half, low, far), ag_recv, (a, 2, half, 0))
            wait_for(slot(a, half, high, far), ag_recv, (a, 2, half, 1))

    gram_rows = pl.ds(pl.multiple_of(x * 128, 128), 128)

    def set_of(s):
        if s == GRAM:
            return gsib_send, gsib_recv, gz_keep, gz_send, gz_recv, gram.at[gram_rows], gpartial
        return (
            sib_send.at[s], sib_recv.at[s], z_keep.at[s], z_send.at[s], z_recv.at[s], rank.at[s], partial,
        )

    def sum_send(s, h, left, a):
        out, into, _, _, _, _, keep = set_of(s)
        n = 1 - c
        out[h] = dot_nt(left, w[a][pl.ds(2 * n, 2)].reshape(256, cols[a])).astype(BF)
        send(out.at[h], into.at[h], ar, (s, h, 0), sibling)
        keep[h] = dot_nt(left, w[a][pl.ds(2 * c, 2)].reshape(256, cols[a]))

    def sum_scatter(s, h):
        _, into, own, out, there, _, keep = set_of(s)
        tall = out.shape[2]
        wait_for(into.at[h], ar_recv, (s, h, 0))
        both = keep[h] + into[h].astype(F32)
        for k in range(NZ):
            zr, zc = k // 2, k % 2
            piece = both[zr * tall : (zr + 1) * tall, zc * 128 : (zc + 1) * 128]
            own[h, k] = piece
            out[h, k] = piece.astype(BF)

        def one(i, carry):
            d = lax.rem(i + 3, NZ - 1) + 1
            start(
                out.at[h, lax.rem(z + d, NZ)], there.at[h, d - 1],
                ar_send.at[s, h, 1], ar_recv.at[s, h, 1], at_z(d),
            )
            return carry

        lax.fori_loop(0, NZ - 1, one, 0, unroll=True)
        sent.append((there.at[h], ar_send, (s, h, 1)))

    def sum_gather(s, h):
        _, _, own, _, there, result, _ = set_of(s)
        tall = own.shape[2]
        wait_for(there.at[h], ar_recv, (s, h, 1))
        total = own[h, z]
        for k in range(NZ - 1):
            total = total + there[h, k].astype(F32)
        row = pl.multiple_of(h * 4 * tall + (z // 2) * tall, 16)
        col = pl.multiple_of(c * 256 + lax.rem(z, 2) * 128, 128)
        mine = result.at[pl.ds(row, tall), pl.ds(col, 128)]
        mine[...] = total.astype(BF)

        def one(i, carry):
            d = lax.rem(i + 3, NZ - 1) + 1
            start(mine, mine, ar_send.at[s, h, 2], ar_recv.at[s, h, 2], at_z(d))
            return carry

        lax.fori_loop(0, NZ - 1, one, 0, unroll=True)
        sent.append((there.at[h], ar_send, (s, h, 2)))

    def half_of(s, h):
        _, _, own, _, _, result, _ = set_of(s)
        tall = own.shape[2]
        col = pl.multiple_of(c * 256, 128)
        return result.at[pl.ds(h * 4 * tall, 4 * tall), pl.ds(col, 256)]

    def sum_share(s, h):
        there = set_of(s)[4]
        wait_for(there.at[h], ar_recv, (s, h, 2))
        part = half_of(s, h)
        send(part, part, ar, (s, h, 3), sibling)

    def sum_end(s, h):
        wait_for(half_of(s, h), ar_recv, (s, h, 3))

    def piece(a, half, t, part):
        return gr[a].at[part, t, 0] if half == 0 else gr[a].at[t, part, 1]

    def add_blocks(out, first, terms, count):
        def one(k, carry):
            total = first(k)[...].astype(F32)
            for term in terms:
                total = total + term(k)[...].astype(F32)
            out(k)[...] = total.astype(BF)
            return carry

        lax.fori_loop(0, count, one, 0)

    def scatter_one(a):
        for half in range(2):
            _, m, _, go = places(half)
            right, far, left = around(m)
            send(piece(a, half, far, low), ra[a].at[half, 0, low], rs, (a, 0, half, 0), go(1))
            send(piece(a, half, far, high), ra[a].at[half, 0, high], rs, (a, 0, half, 1), go(3))
            send(piece(a, half, right, high), ra[a].at[half, 1, high], rs, (a, 1, half, 0), go(1))
            send(piece(a, half, left, low), ra[a].at[half, 1, low], rs, (a, 1, half, 1), go(3))

    def scatter_mid(a):
        for half in range(2):
            _, m, _, go = places(half)
            right, _, left = around(m)
            for side, (part, base, to, d) in enumerate(((low, 0, right, 1), (high, 2, left, 3))):
                wait_for(ra[a].at[half, 0, part], rs_recv, (a, 0, half, side))
                add_blocks(
                    lambda k: cb[a].at[half, base + k],
                    lambda k: piece(a, half, to, base + k),
                    (lambda k: ra[a].at[half, 0, base + k],),
                    2,
                )
                send(cb[a].at[half, part], ra[a].at[half, 2, part], rs, (a, 2, half, side), go(d))

    def scatter_two(a):
        for half in range(2):
            q, m, go, _ = places(half)
            wait_for(ra[a].at[half, 1, high], rs_recv, (a, 1, half, 0))
            wait_for(ra[a].at[half, 1, low], rs_recv, (a, 1, half, 1))
            wait_for(ra[a].at[half, 2, low], rs_recv, (a, 2, half, 0))
            wait_for(ra[a].at[half, 2, high], rs_recv, (a, 2, half, 1))
            add_blocks(
                lambda k: rb[a].at[half, k],
                lambda k: piece(a, half, m, k),
                (lambda k: ra[a].at[half, 1, k], lambda k: ra[a].at[half, 2, k]),
                4,
            )
            for d in (2, 1, 3):
                send(
                    rb[a].at[half, lax.rem(q + d, 4)], rc[a].at[half, d - 1],
                    rs, (a, 3, half, d - 1), go(d),
                )

    def scatter_near(a):
        left_cols, right_cols = cut(a)
        for half in range(2):
            q, m, go, _ = places(half)
            wait_for(ra[a].at[half, 1, high], rs_recv, (a, 1, half, 0))
            wait_for(ra[a].at[half, 1, low], rs_recv, (a, 1, half, 1))
            wait_for(ra[a].at[half, 2, low], rs_recv, (a, 2, half, 0))
            wait_for(ra[a].at[half, 2, high], rs_recv, (a, 2, half, 1))
            add_blocks(
                lambda k: rb[a].at[half, k],
                lambda k: piece(a, half, m, k),
                (lambda k: ra[a].at[half, 1, k], lambda k: ra[a].at[half, 2, k]),
                4,
            )
            right, far, left = around(q)
            for kind, side, owner, part, d in (
                (0, 0, far, left_cols, 1),
                (0, 1, far, right_cols, 3),
                (1, 0, right, right_cols, 1),
                (1, 1, left, left_cols, 3),
            ):
                send(
                    rb[a].at[half, owner, :, part], rc[a].at[half, kind, :, part],
                    rs, (a, 3 + kind, half, side), go(d),
                )

    def scatter_late(a):
        left_cols, right_cols = cut(a)
        for half in range(2):
            q, _, go, _ = places(half)
            right, _, left = around(q)
            for side, (part, owner, d) in enumerate(((left_cols, right, 1), (right_cols, left, 3))):
                wait_for(rc[a].at[half, 0, :, part], rs_recv, (a, 3, half, side))
                total = rb[a][half, owner, :, part].astype(F32) + rc[a][half, 0, :, part].astype(F32)
                cc[a][half, :, part] = total.astype(BF)
                send(
                    cc[a].at[half, :, part], rc[a].at[half, 2, :, part],
                    rs, (a, 5, half, side), go(d),
                )

    def scatter_done(a):
        left_cols, right_cols = cut(a)
        squares = jnp.zeros((8, 128), F32)
        for half in range(2):
            q, _, _, _ = places(half)
            wait_for(rc[a].at[half, 1, :, right_cols], rs_recv, (a, 4, half, 0))
            wait_for(rc[a].at[half, 1, :, left_cols], rs_recv, (a, 4, half, 1))
            wait_for(rc[a].at[half, 2, :, left_cols], rs_recv, (a, 5, half, 0))
            wait_for(rc[a].at[half, 2, :, right_cols], rs_recv, (a, 5, half, 1))
            total = rb[a][half, q].astype(F32) + rc[a][half, 1].astype(F32) + rc[a][half, 2].astype(F32)
            gouts[a][half * 16 : (half + 1) * 16, :] = total
            sq = total * total
            sq = sq[0:8] + sq[8:16]
            for j in range(cols[a] // 128):
                squares = squares + sq[:, j * 128 : (j + 1) * 128]
        return squares

    def scatter_end(a):
        squares = jnp.zeros((8, 128), F32)
        for half in range(2):
            q, _, _, _ = places(half)
            total = rb[a][half, q].astype(F32)
            for d in range(3):
                wait_for(rc[a].at[half, d], rs_recv, (a, 3, half, d))
                total = total + rc[a][half, d].astype(F32)
            gouts[a][half * 16 : (half + 1) * 16, :] = total
            sq = total * total
            sq = sq[0:8] + sq[8:16]
            for j in range(cols[a] // 128):
                squares = squares + sq[:, j * 128 : (j + 1) * 128]
        return squares

    def gradient(a, left, right):
        ranks_t[...] = left[...].T
        step = 768 if cols[a] % 768 == 0 else 384

        def one(j, carry):
            at = pl.ds(pl.multiple_of(j * step, 128), step)
            tile = dot_nn(ranks_t[...], right[:, at]).astype(BF)
            gr[a][:, :, :, :, at] = tile.reshape(NX, NY, 2, 16, step)
            return carry

        lax.fori_loop(0, cols[a] // step, one, 0)

    def tile_of(a, at, n):
        return w[a][:, :, :, :, at].reshape(RANK, n)

    def rows_of(h):
        return pl.ds(h * HALF, HALF)

    def stage_zero(h):
        sum_send(0, h, tok[rows_of(h), :], PI)

    def stage_one(h):
        left = rank[0, rows_of(h), :]

        def one(j, carry):
            at = pl.ds(pl.multiple_of(j * 768, 128), 768)
            pre = jnp.maximum(dot_nn(left, tile_of(PO, at, 768)), 0.0)
            relu[rows_of(h), at] = pre
            hid[rows_of(h), at] = (pre * pre).astype(BF)
            return carry

        lax.fori_loop(0, cols[PO] // 768, one, 0)

    def stage_two(h):
        left = rank[1, rows_of(h), :]

        def one(j, carry):
            at = pl.ds(pl.multiple_of(j * 384, 128), 384)
            misfit = dot_nn(left, tile_of(QO, at, 384)) - tgt[rows_of(h), at].astype(F32)
            gout[rows_of(h), at] = (misfit * (1.0 / TOTAL)).astype(BF)
            sq = (misfit * misfit).reshape(HALF // 8, 8, 384).sum(axis=0)
            loss_acc[...] += sq[:, 0:128] + sq[:, 128:256] + sq[:, 256:384]
            return carry

        lax.fori_loop(0, cols[QO] // 384, one, 0)

    def stage_back(h):
        up = dot_nn(rank[1, rows_of(h), :], gram[...]) - rank[2, rows_of(h), :].astype(F32)
        back[rows_of(h), :] = (up * (1.0 / TOTAL)).astype(BF)

    def stage_three(h):
        left = back[rows_of(h), :]

        def one(j, carry):
            at = pl.ds(pl.multiple_of(j * 768, 128), 768)
            up = dot_nn(left, tile_of(QI, at, 768))
            gpre[rows_of(h), at] = (up * 2.0 * relu[rows_of(h), at]).astype(BF)
            return carry

        lax.fori_loop(0, cols[QI] // 768, one, 0)

    def gram_send():
        sum_send(GRAM, 0, w[QO][x].reshape(128, cols[QO]), QO)

    def gram_spread():
        part = gram.at[gram_rows]
        for d in (2, 1, 3):
            send(part, part, (gr_send, gr_recv), (d - 1,), at_x(d))

    def gram_end():
        for d in range(3):
            wait_for(gram.at[gram_rows], gr_recv, (d,))

    loss_acc[...] = jnp.zeros_like(loss_acc)
    loads[0].wait()
    cast(PI)
    pl.semaphore_wait(barrier, 2 * (DP - 1))
    gather_one(PI)
    loads[4].wait()
    cast(QO)
    gather_one(QO)
    loads[1].wait()
    cast(PO)
    gather_two(PI)
    gather_two(QO)
    gather_one(PO)
    loads[3].wait()
    cast(QI)
    gather_last(PI)
    gather_last(QO)
    gather_two(PO)
    gather_one(QI)
    loads[2].wait()
    loads[5].wait()
    gather_end(PI)
    stage_zero(0)
    sum_scatter(0, 0)
    stage_zero(1)
    sum_scatter(0, 1)
    sum_gather(0, 0)
    sum_gather(0, 1)
    gather_last(PO)
    gather_all(QI)
    gather_end(QO)
    gram_send()
    sum_scatter(GRAM, 0)
    sum_send(2, 0, tgt[rows_of(0), :], QO)
    sum_scatter(2, 0)
    sum_send(2, 1, tgt[rows_of(1), :], QO)
    sum_scatter(2, 1)
    sum_share(0, 0)
    sum_share(0, 1)
    sum_gather(2, 0)
    sum_gather(2, 1)
    sum_gather(GRAM, 0)
    gather_end(PO)
    sum_end(0, 0)
    stage_one(0)
    sum_end(0, 1)
    stage_one(1)
    sum_share(2, 0)
    sum_share(2, 1)
    sum_share(GRAM, 0)
    gather_done(QI)
    sum_send(1, 0, hid[rows_of(0), :], QI)
    sum_scatter(1, 0)
    sum_send(1, 1, hid[rows_of(1), :], QI)
    sum_scatter(1, 1)
    sum_end(GRAM, 0)
    gram_spread()
    sum_gather(1, 0)
    sum_gather(1, 1)
    sum_end(2, 0)
    sum_end(2, 1)
    gram_end()
    sum_share(1, 0)
    sum_end(1, 0)
    stage_two(0)
    stage_back(0)
    sum_share(1, 1)
    sum_end(1, 1)
    stage_two(1)
    gradient(QO, rank.at[1], gout)
    scatter_one(QO)
    stage_back(1)
    gradient(QI, back, hid)
    scatter_one(QI)
    stage_three(0)
    sum_send(3, 0, gpre[rows_of(0), :], PO)
    sum_scatter(3, 0)
    stage_three(1)
    sum_send(3, 1, gpre[rows_of(1), :], PO)
    sum_scatter(3, 1)
    scatter_mid(QO)
    gradient(PO, rank.at[0], gpre)
    scatter_one(PO)
    sum_gather(3, 0)
    sum_gather(3, 1)
    scatter_mid(QI)
    sum_share(3, 0)
    sum_share(3, 1)
    scatter_near(QO)
    sum_end(3, 0)
    sum_end(3, 1)
    gradient(PI, rank.at[3], tok)
    scatter_one(PI)
    scatter_late(QO)
    scatter_mid(PO)
    scatter_near(QI)
    scatter_mid(PI)
    scatter_near(PO)
    scatter_late(QI)
    squares = scatter_done(QO)
    scatter_two(PI)
    scatter_late(PO)
    squares = squares + scatter_done(QI)
    squares = squares + scatter_done(PO)
    squares = squares + scatter_end(PI)

    sc_buf[0, me_t, 0] = squares
    sc_buf[0, me_t, 1] = loss_acc[...]

    def over_tensor(k, carry):
        own = sc_buf.at[0, me_t]
        start(own, own, sc_send.at[0], sc_recv.at[0], (me_dp, lax.rem(me_t + k, TP)))
        return carry

    lax.fori_loop(1, TP, over_tensor, 0, unroll=True)
    for ref, sem, spot_of in sent:
        wait_for(ref, sem, spot_of)
    wait_for(sc_buf.at[0, pl.ds(0, TP - 1)], sc_recv, (0,))
    sc_buf[1, me_dp] = jnp.sum(sc_buf[0], axis=0)

    def over_dp(k, carry):
        own = sc_buf.at[1, me_dp]
        start(own, own, sc_send.at[1], sc_recv.at[1], (lax.rem(me_dp + k, DP), me_t))
        return carry

    lax.fori_loop(1, DP, over_dp, 0, unroll=True)
    wait_for(sc_buf.at[1, pl.ds(0, DP - 1)], sc_recv, (1,))
    stat[...] = jnp.sum(sc_buf[1], axis=0)

    for k in range(2):
        wait_for(sc_buf.at[k, pl.ds(0, TP - 1)], sc_send, (k,))


def adam_body(
    stat, g_pi, g_po, g_qi, g_qo, p_pi, p_po, p_qi, p_qo, wm, ws, hm, hs,
    n_pi, n_po, n_qi, n_qo, nwm, nws, nhm, nhs, loss,
):
    squares = jnp.sum(stat[0])
    scale = 1.0 / jnp.maximum(jnp.sqrt(squares), 1.0)
    loss[0, 0] = jnp.sum(stat[1]) / (2.0 * TOTAL)
    for g, p, m, v, k, new_p, new_m, new_v in (
        (g_pi, p_pi, wm, ws, 0, n_pi, nwm, nws),
        (g_qo, p_qo, wm, ws, 1, n_qo, nwm, nws),
        (g_po, p_po, hm, hs, 0, n_po, nhm, nhs),
        (g_qi, p_qi, hm, hs, 1, n_qi, nhm, nhs),
    ):
        grad = g[...] * scale
        mean = beta_one * m[k] + (1.0 - beta_one) * grad
        square = beta_two * v[k] + (1.0 - beta_two) * grad * grad
        corrected = mean * (1.0 / (1.0 - beta_one**10))
        spread = jnp.sqrt(square * (1.0 / (1.0 - beta_two**10))) + tiny_eps
        new_p[...] = p[...] - learn_rate * corrected / spread
        new_m[k] = mean
        new_v[k] = square


def shards(
    tokens, target, first_in, first_out, second_in, second_out,
    width_mean, width_square, hidden_mean, hidden_square,
):
    wide = first_in.shape[1]
    deep = first_out.shape[1]
    cols = (wide, deep, deep, wide)
    vm = pltpu.VMEM
    dma = pltpu.SemaphoreType.DMA
    scratch = [vm((TOKD, wide), BF), vm((TOKD, wide), BF)]
    scratch += [vm((ROWS, n), F32) for n in cols]
    scratch += [vm((NX, NY, 2, 16, n), BF) for n in cols]
    scratch += [vm((NX, NY, 2, 16, n), BF) for n in cols]
    scratch += [vm((2, 3, 4, 16, n), BF) for n in cols]
    scratch += [vm((2, 4, 16, n), BF) for n in cols]
    scratch += [vm((2, 3, 16, n), BF) for n in cols]
    scratch += [vm((2, 4, 16, n), BF) for n in cols]
    scratch += [vm((2, 16, n), BF) for n in cols]
    scratch += [
        vm((4, TOKD, RANK), BF),
        vm((TOKD, RANK), BF),
        vm((RANK, TOKD), BF),
        vm((TOKD, deep), F32),
        vm((TOKD, deep), BF),
        vm((TOKD, deep), BF),
        vm((TOKD, wide), BF),
        vm((2, HALF, 256), F32),
        vm((4, 2, HALF, 256), BF),
        vm((4, 2, HALF, 256), BF),
        vm((4, 2, NZ, 48, 128), F32),
        vm((4, 2, NZ, 48, 128), BF),
        vm((4, 2, NZ - 1, 48, 128), BF),
        vm((RANK, RANK), BF),
        vm((1, 128, 256), F32),
        vm((1, 128, 256), BF),
        vm((1, 128, 256), BF),
        vm((1, NZ, 32, 128), F32),
        vm((1, NZ, 32, 128), BF),
        vm((1, NZ - 1, 32, 128), BF),
        vm((8, 128), F32),
        vm((2, 16, 2, 8, 128), F32),
        dma((6,)),
        dma((4, 3, 2, 3)), dma((4, 3, 2, 3)),
        dma((4, 6, 2, 3)), dma((4, 6, 2, 3)),
        dma((5, 2, 4)), dma((5, 2, 4)),
        dma((3,)), dma((3,)),
        dma((2,)), dma((2,)),
    ]
    whole = pl.BlockSpec(memory_space=pltpu.VMEM)
    g_pi, g_po, g_qi, g_qo, stat = pl.pallas_call(
        body,
        name="step",
        out_shape=[jax.ShapeDtypeStruct((ROWS, n), F32) for n in cols]
        + [jax.ShapeDtypeStruct((2, 8, 128), F32)],
        in_specs=[pl.BlockSpec(memory_space=pl.ANY)] * 6,
        out_specs=[whole] * 5,
        scratch_shapes=scratch,
        compiler_params=pltpu.CompilerParams(
            collective_id=0, has_side_effects=True, vmem_limit_bytes=58 * 2**20
        ),
    )(tokens, target, first_in, first_out, second_in, second_out)

    outs = pl.pallas_call(
        adam_body,
        name="adam",
        out_shape=[jax.ShapeDtypeStruct((ROWS, n), F32) for n in cols]
        + [jax.ShapeDtypeStruct((2, ROWS, n), F32) for n in (wide, wide, deep, deep)]
        + [jax.ShapeDtypeStruct((1, 1), F32)],
        in_specs=[whole] * 13,
        out_specs=[whole] * 8 + [pl.BlockSpec(memory_space=pltpu.SMEM)],
        compiler_params=pltpu.CompilerParams(vmem_limit_bytes=60 * 2**20),
    )(
        stat, g_pi, g_po, g_qi, g_qo, first_in, first_out, second_in, second_out,
        width_mean, width_square, hidden_mean, hidden_square,
    )
    return tuple(outs[:8]) + (outs[8].reshape(()),)


def solution(mesh):
    two = P("dp", "tensor")
    three = P(None, "dp", "tensor")
    return jax.shard_map(
        shards,
        mesh=mesh,
        in_specs=(two,) * 6 + (three,) * 4,
        out_specs=(two,) * 4 + (three,) * 4 + (P(),),
        check_vma=False,
    )
```
